256 devices in a mesh: section: 2 (over x_hi), tensor: 2 (over core), dp: 64 (over z, y, x_lo).
Axes of the slice: x: 4 (x_hi: 2, x_lo: 2; x = x_hi * 2 + x_lo), y: 4, z: 8, core: 2. Of those that a mesh axis runs over, the one named last changes fastest.
Arguments:
- layer_input: bfloat16 [2, 16384, 4096], P('section', 'dp', 'tensor')
- other_grad: bfloat16 [2, 16384, 4096], P('section', 'dp', 'tensor'), may hold values from -3 to 3
- head_grad: bfloat16 [2, 16384, 2048], P('section', 'dp', 'tensor')
- lengths: int32 [256], P('dp'), may hold values from 1 to 64, 10922 in all
- proj_weight: bfloat16 [2, 4096, 2048], P('section', None, 'tensor'), may hold values from -0.09375 to 0.09375
- old_momentum: bfloat16 [2, 4096, 2048], P('section', None, 'tensor'), may hold values from -5 to 5
Outputs:
- upstream_grad: bfloat16 [2, 16384, 4096], P('section', 'dp', 'tensor')
- momentum: bfloat16 [2, 4096, 2048], P('section', None, 'tensor')
- worker_error: bfloat16 [2, 64, 4096, 2048], P('section', 'dp', None, 'tensor')
- server_error: float32 [2, 4096, 2048], P('section', 'dp', 'tensor')
The draws below stay inside these ranges and needn't reach their ends.
Inputs may be any that keep to these rules, and one draw needn't show every extreme that they name: `lengths`: each sequence's length; some sequence has all 64 slots used.
All inputs are finite; a program needn't handle non-finite values. Where the reference program divides by a largest or mean magnitude, that divisor is 1e-20 or more. No bound on the sum of `lengths` on one device may be relied on, other than what follows from the above.
Results may differ from the reference program's by a relative error of at most 0.02.
Values may be sent and summed in bfloat16 or wider, within the bound.
No kernel may reach another device: no remote copies, remote signals or barrier semaphores. Data moves between devices by JAX's collectives and lax.ppermute only.
A program may use at most 192 MiB of HBM per device.

```python
import math
import jax
import jax.numpy as jnp
import numpy as np
from jax import lax

D = 4096
HEAD = 128
KV_HEADS = 8
SLOT = 64
TOK_DEV = 256
SEQS = 256
TOKENS = 16384
KVW = 2048
SPAN = 64
N_SECTION = 2
N_DP = 64


def heavy_blocks(key):
    keys = jax.random.split(key, 6)
    targets = jnp.arange(N_DP, dtype=jnp.int32)
    marks = jnp.zeros((N_DP, N_DP), jnp.float32)
    for index in range(6):
        orders = jax.random.permutation(keys[index], N_DP).astype(jnp.int32)
        marks = jnp.maximum(marks, jnp.where(orders[:, None] == targets[None, :], 1.0, 0.0))
    return 1.0 + 23.0 * marks


def draw_layer_input(key, part):
    key = jax.random.fold_in(key, 11)
    key_base = jax.random.fold_in(key, 0)
    key_feat = jax.random.fold_in(key, 1)
    key_pair = jax.random.fold_in(key, 3)
    feature_scale = 10.0 ** jax.random.uniform(key_feat, (1, 1, D), dtype=jnp.float32) / 3.0
    values = jax.random.normal(key_base, (N_SECTION, TOKENS, D), dtype=jnp.float32) * feature_scale
    factor = heavy_blocks(key_pair)
    values = values.reshape(N_SECTION, N_DP, TOK_DEV, N_DP, SPAN) * factor[None, :, None, :, None]
    return values.reshape(N_SECTION, TOKENS, D).astype(jnp.bfloat16)


def draw_head_grad(key, part):
    key = jax.random.fold_in(key, 23)
    key_base, key_cols, key_heads = jax.random.split(key, 3)
    order = jax.random.permutation(key_heads, KV_HEADS).astype(jnp.float32)
    head_scale = 3.0 ** (order / (KV_HEADS - 1))
    column_head = jnp.arange(KVW, dtype=jnp.int32) // (2 * HEAD)
    picked = jnp.sum(jnp.where(column_head[:, None] == jnp.arange(KV_HEADS, dtype=jnp.int32)[None, :], head_scale[None, :], 0.0), axis=1)
    column_scale = 10.0 ** jax.random.uniform(key_cols, (KVW,), dtype=jnp.float32) / 30.0
    scales = (picked * column_scale)[None, None, :]
    values = jax.random.normal(key_base, (N_SECTION, TOKENS, KVW), dtype=jnp.float32) * scales
    return values.astype(jnp.bfloat16)


def steps_of(rng, extent, pieces, smallest, largest):
    factor_of = 1.0
    for position, shards_of in pieces:
        heights = jax.random.uniform(jax.random.fold_in(jax.random.fold_in(rng, 6), position), (shards_of,), jnp.float32, smallest / len(pieces), largest / len(pieces))
        factor_of = factor_of * jnp.repeat(jnp.exp(heights), extent[position] // shards_of).reshape((-1,) + (1,) * (len(extent) - 1 - position))
    return factor_of


def split_up(number_of, total, limit, lean):
    loads = [(1 << 20) // math.isqrt(standing ** lean) + 1 for standing in range(2, number_of + 1)]
    surplus, holding = total - limit - (number_of - 1), [1] * (number_of - 1)
    while surplus > 0:
        movable = [i for i in range(number_of - 1) if holding[i] < limit]
        whole, remaining = sum([loads[i] for i in movable]), surplus
        for i in movable:
            more = min(limit - holding[i], max(1, remaining * loads[i] // whole), surplus)
            holding[i] = holding[i] + more
            surplus = surplus - more
    return np.array([limit] + holding)


def uneven(key, count, total, limit, slope):
    if count == 2:
        one = jax.random.randint(key, (), max(1, total - limit), min(limit, total - 1) + 1)
        return jnp.stack([one, total - one])
    sizes = jnp.asarray(split_up(count, total, limit, slope), jnp.int32)
    twos = (count - 1) // 2
    giver, sink = sizes[1:1 + 2 * twos:2], sizes[2:2 + 2 * twos:2]
    slack = jnp.minimum(giver - 1, limit - sink)
    passed = jax.random.randint(jax.random.fold_in(key, 1), (twos,), 0, 1 << 20) % (slack + 1)
    sizes = sizes.at[1:1 + 2 * twos:2].set(giver - passed).at[2:2 + 2 * twos:2].set(sink + passed)
    return sizes[jax.random.permutation(jax.random.fold_in(key, 2), count)]


def noise(key, dims, scale, limit, shards=(), kind=jnp.bfloat16):
    factor_of = steps_of(key, dims, shards, -0.22, 0.18) if shards else 1.0
    array = jax.random.normal(key, dims, jnp.float32) * scale * factor_of
    return jnp.minimum(jnp.maximum(array, -limit), limit).astype(kind)


def setup_inputs(seed: int = 0) -> dict:
    key_of = jax.random.split(jax.random.key(seed), 7)
    return {
        "layer_input": draw_layer_input(jax.random.fold_in(key_of[6], 71), 0),
        "other_grad": noise(key_of[1], (N_SECTION, TOKENS, D), 0.5, 3.0, ((0, 2), (1, 64), (2, 2))),
        "head_grad": draw_head_grad(jax.random.fold_in(key_of[6], 71), 0),
        "lengths": uneven(key_of[3], SEQS, SEQS * SLOT * 2 // 3, SLOT, 1).astype(jnp.int32),
        "proj_weight": noise(key_of[4], (N_SECTION, D, KVW), D ** -0.5, 0.09375, ((0, 2), (2, 2))),
        "old_momentum": noise(key_of[5], (N_SECTION, D, KVW), 1.0, 5.0, ((0, 2), (2, 2))),
    }


momentum_decay = 0.9
saturation = 0.5
epsilon_term = 1e-6


def compress(values, axes):
    scales = jnp.mean(jnp.abs(values), axis=axes, keepdims=True)
    clipped = jnp.clip(values / (saturation * scales + epsilon_term), -1.0, 1.0)
    return (scales * clipped).astype(jnp.bfloat16)


def reference(layer_input, other_grad, head_grad, lengths, proj_weight, old_momentum):
    positions = jnp.arange(TOKENS, dtype=jnp.int32)
    limits = jnp.take(lengths, (positions // SLOT).astype(jnp.int32))
    valid_mask = (positions % SLOT) < limits
    used_grad = jnp.where(valid_mask[None, :, None], head_grad, jnp.zeros_like(head_grad))
    terms = []
    momenta = []
    worker_list = []
    server_list = []
    for section_index in range(N_SECTION):
        partial_sum = lax.dot_general(used_grad[section_index], proj_weight[section_index], (((1,), (1,)), ((), ())), preferred_element_type=jnp.float32)
        terms.append(other_grad[section_index].astype(jnp.float32) + partial_sum)
        inputs_wide = layer_input[section_index].reshape(N_DP, TOK_DEV, D).astype(jnp.float32)
        grads_wide = used_grad[section_index].reshape(N_DP, TOK_DEV, KVW).astype(jnp.float32)
        weight_grad = jnp.einsum("rtd,rtk->rdk", inputs_wide, grads_wide)
        local_momentum = momentum_decay * old_momentum[section_index].astype(jnp.float32)[None] + (1.0 - momentum_decay) * weight_grad
        blocks = local_momentum.reshape(N_DP, N_DP, SPAN, KVW)
        compressed = compress(blocks, (2, 3))
        worker_list.append((blocks - compressed.astype(jnp.float32)).astype(jnp.bfloat16).reshape(N_DP, D, KVW))
        averaged = jnp.mean(compressed.astype(jnp.float32), axis=0)
        owned = compress(averaged, (1, 2))
        server_list.append((averaged - owned.astype(jnp.float32)).reshape(D, KVW))
        momenta.append(owned.reshape(D, KVW))
    stacked = jnp.stack(terms)
    suffix = jnp.flip(jnp.cumsum(jnp.flip(stacked, 0), axis=0), 0)
    return (suffix.astype(jnp.bfloat16), jnp.stack(momenta), jnp.stack(worker_list), jnp.stack(server_list))
```

```python
import functools

import jax
import jax.numpy as jnp
from jax import lax
from jax.experimental import pallas as pl
from jax.experimental.pallas import tpu as pltpu
from jax.sharding import Mesh, PartitionSpec as P

momentum_decay = 0.9
saturation = 0.5
epsilon_term = 1e-06

Z, Y, X = 8, 4, 2
SPAN = 64
COLS_Y, COLS_X = 384, 128
F32, BF16 = jnp.float32, jnp.bfloat16
PARAMS = pltpu.CompilerParams(vmem_limit_bytes=48 * 1024 * 1024)
ANY = pl.BlockSpec(memory_space=pl.ANY)


def local_block(x, g, m):
    grad = lax.dot_general(x, g, (((0,), (0,)), ((), ())), preferred_element_type=F32)
    return momentum_decay * m.astype(F32) + (1.0 - momentum_decay) * grad


def sums_kernel(where_ref, x_ref, g_ref, m_ref, out_ref):
    local = jnp.abs(local_block(x_ref[...], g_ref[...], m_ref[...]))
    rows, cols = local.shape
    per_span = jnp.sum(local.reshape(rows // SPAN, SPAN, cols), axis=1)
    total = per_span[:, :128]
    for lane in range(128, cols, 128):
        total = total + per_span[:, lane : lane + 128]
    out_ref[...] = total


def block_sums(x, g, m, first):
    tokens, feats = x.shape
    cols = g.shape[1]
    rows = Y * X * SPAN
    steps = feats // rows
    return pl.pallas_call(
        sums_kernel,
        grid_spec=pltpu.PrefetchScalarGridSpec(
            num_scalar_prefetch=1,
            grid=(steps,),
            in_specs=[
                pl.BlockSpec((tokens, rows), lambda i, w: (0, i)),
                pl.BlockSpec((tokens, cols), lambda i, w: (0, 0)),
                pl.BlockSpec((rows, cols), lambda i, w: (w[0] + i, 0)),
            ],
            out_specs=pl.BlockSpec((rows // SPAN, 128), lambda i, w: (i, 0)),
        ),
        out_shape=jax.ShapeDtypeStruct((feats // SPAN, 128), F32),
        compiler_params=PARAMS,
        cost_estimate=pl.CostEstimate(
            flops=2 * tokens * feats * cols, bytes_accessed=2 * feats * cols, transcendentals=0
        ),
    )(first.reshape(1), x, g, m)


def squash(local, scale):
    slope = scale / (saturation * scale + epsilon_term)
    return jnp.clip(local * slope, -scale, scale).astype(BF16)


def compress_kernel(half, col, where_ref, own_ref, other_ref, g_ref, m_ref, s_ref, *rest):
    step = pl.program_id(0)
    x = jnp.where(step < half, own_ref[...], other_ref[...])
    local = local_block(x, g_ref[...], m_ref[...])
    if col == 0:
        err_ref, a_ref = rest
    else:
        _, err_ref, y_ref, x_ref = rest
    my_y, my_x = where_ref[1], where_ref[2]
    for j in range(Y * X):
        part = local[j * SPAN : (j + 1) * SPAN]
        packed = squash(part, s_ref[j : j + 1, 0:1])
        err_ref[j * SPAN : (j + 1) * SPAN] = (part - packed.astype(F32)).astype(BF16)
        if col == 0:
            a_ref[j * SPAN : (j + 1) * SPAN] = packed
        else:
            dy = lax.rem(j // X - my_y + Y, Y)
            dx = lax.rem(j % X - my_x + X, X)
            y_ref[dy, dx, 0] = packed[:, :COLS_Y]
            x_ref[dx, dy, 0] = packed[:, COLS_Y:]


def compress(own, other, g, m, scales, where, col, err=None):
    tokens, feats = own.shape
    width, cols = m.shape
    rows = Y * X * SPAN
    half = feats // rows
    cut = cols // 2
    in_specs = [
        pl.BlockSpec((tokens, rows), lambda i, w: (0, jnp.minimum(i, half - 1))),
        pl.BlockSpec((tokens, rows), lambda i, w: (0, jnp.maximum(i - half, 0))),
        pl.BlockSpec((tokens, cut), lambda i, w: (0, col)),
        pl.BlockSpec((rows, cut), lambda i, w: (lax.rem(w[0] + i, 2 * half), col)),
        pl.BlockSpec((rows // SPAN, 128), lambda i, w: (lax.rem(w[0] + i, 2 * half), 0)),
    ]
    operands = [own, other, g, m, scales]
    out_specs = [pl.BlockSpec((rows, cut), lambda i, w: (lax.rem(w[0] + i, 2 * half), col))]
    out_shape = [jax.ShapeDtypeStruct((width, cols), BF16)]
    aliases = {}
    if col == 0:
        out_specs += [pl.BlockSpec((rows, cut), lambda i, w: (lax.rem(w[0] + i, 2 * half), 0))]
        out_shape += [jax.ShapeDtypeStruct((width, cut), BF16)]
    else:
        in_specs += [ANY]
        operands += [err]
        aliases = {6: 0}
        out_specs += [
            pl.BlockSpec((Y, X, 1, SPAN, COLS_Y), lambda i, w: (0, 0, lax.rem(w[0] + i, 2 * half), 0, 0)),
            pl.BlockSpec((X, Y, 1, SPAN, COLS_X), lambda i, w: (0, 0, lax.rem(w[0] + i, 2 * half), 0, 0)),
        ]
        out_shape += [
            jax.ShapeDtypeStruct((Y, X, Z, SPAN, COLS_Y), BF16),
            jax.ShapeDtypeStruct((X, Y, Z, SPAN, COLS_X), BF16),
        ]
    return pl.pallas_call(
        functools.partial(compress_kernel, half, col),
        grid_spec=pltpu.PrefetchScalarGridSpec(
            num_scalar_prefetch=1, grid=(2 * half,), in_specs=in_specs, out_specs=out_specs
        ),
        out_shape=out_shape,
        input_output_aliases=aliases,
        compiler_params=PARAMS,
        cost_estimate=pl.CostEstimate(
            flops=2 * tokens * width * cut, bytes_accessed=6 * width * cut, transcendentals=0
        ),
    )(where, *operands)


def input_grad_kernel(half, where_ref, g_ref, w_ref, after_ref, own_ref, other_ref):
    step = pl.program_id(0)
    term = lax.dot_general(g_ref[...], w_ref[...], (((1,), (1,)), ((), ())), preferred_element_type=F32)

    @pl.when(step < half)
    def _():
        other_ref[...] = term

    @pl.when(step >= half)
    def _():
        own_ref[...] = term


def input_grad(g, weight, first_other, after):
    tokens, cols = g.shape
    width = weight.shape[0]
    rows = min(512, width // 2)
    half = width // 2 // rows
    return pl.pallas_call(
        functools.partial(input_grad_kernel, half),
        grid_spec=pltpu.PrefetchScalarGridSpec(
            num_scalar_prefetch=1,
            grid=(2 * half,),
            in_specs=[
                pl.BlockSpec((tokens, cols), lambda i, w: (0, 0)),
                pl.BlockSpec((rows, cols), lambda i, w: (lax.rem(w[0] * half + i, 2 * half), 0)),
                ANY,
            ],
            out_specs=[
                pl.BlockSpec((tokens, rows), lambda i, w: (0, jnp.maximum(i - half, 0))),
                pl.BlockSpec((tokens, rows), lambda i, w: (0, jnp.minimum(i, half - 1))),
            ],
        ),
        out_shape=[jax.ShapeDtypeStruct((tokens, width // 2), F32)] * 2,
        compiler_params=PARAMS,
        cost_estimate=pl.CostEstimate(
            flops=2 * tokens * width * cols,
            bytes_accessed=2 * width * cols + 4 * tokens * width,
            transcendentals=0,
        ),
    )(first_other.reshape(1), g, weight, after)


def assemble_kernel(where_ref, a_ref, *rest):
    y_refs, x_refs, out_ref = rest[:Y], rest[Y : Y + X], rest[Y + X]
    cut = a_ref.shape[1]
    out_ref[:, :cut] = a_ref[...]
    my_y, my_x = where_ref[1], where_ref[2]
    for dy in range(Y):
        for dx in range(X):
            j = lax.rem(my_y + dy, Y) * X + lax.rem(my_x + dx, X)
            rows = pl.ds(pl.multiple_of(j * SPAN, SPAN), SPAN)
            out_ref[rows, cut : cut + COLS_Y] = y_refs[dy][dx, 0]
            out_ref[rows, cut + COLS_Y :] = x_refs[dx][dy, 0]


def assemble(where, a, y_parts, x_parts):
    width, cut = a.shape
    rows = Y * X * SPAN
    return pl.pallas_call(
        assemble_kernel,
        grid_spec=pltpu.PrefetchScalarGridSpec(
            num_scalar_prefetch=1,
            grid=(Z,),
            in_specs=[pl.BlockSpec((rows, cut), lambda i, w: (i, 0))]
            + [pl.BlockSpec((X, 1, SPAN, COLS_Y), lambda i, w: (0, i, 0, 0))] * Y
            + [pl.BlockSpec((Y, 1, SPAN, COLS_X), lambda i, w: (0, i, 0, 0))] * X,
            out_specs=pl.BlockSpec((rows, 2 * cut), lambda i, w: (i, 0)),
        ),
        out_shape=jax.ShapeDtypeStruct((width, 2 * cut), BF16),
        compiler_params=PARAMS,
        cost_estimate=pl.CostEstimate(flops=0, bytes_accessed=8 * width * cut, transcendentals=0),
    )(where, a, *y_parts, *x_parts)


def turned(value, axis, steps):
    count = lax.axis_size(axis)
    return lax.ppermute(value, axis, [(i, (i + steps) % count) for i in range(count)])


def shards(layer_input, other_grad, head_grad, lengths, proj_weight, old_momentum):
    tensor = lax.axis_index("tensor").astype(jnp.int32)
    my_y = lax.axis_index("y").astype(jnp.int32)
    my_x = lax.axis_index("x").astype(jnp.int32)
    own, momentum, weight = layer_input[0], old_momentum[0], proj_weight[0]
    width, cols = momentum.shape
    cut = cols // 2
    other = turned(own, "tensor", 1)

    seq_count = lengths.shape[0]
    slot_len = own.shape[0] // seq_count
    slot_index = lax.broadcasted_iota(jnp.int32, (seq_count, slot_len), 1)
    valid_mask = (slot_index < lengths[:, None]).reshape(-1, 1)
    used_grad = jnp.where(valid_mask, head_grad[0], jnp.zeros_like(head_grad[0]))

    half = width // 2 // (Y * X * SPAN)
    own_sums = block_sums(own, used_grad, momentum, tensor * half)
    other_sums = block_sums(other, used_grad, momentum, (1 - tensor) * half)
    stacked = jnp.stack([own_sums, other_sums])
    both = jnp.where(tensor == 0, stacked, stacked[::-1]).sum(axis=2).reshape(-1)
    scales = lax.psum(both, "tensor") / (SPAN * cols * 2)
    scales = jnp.broadcast_to(scales[:, None], (scales.shape[0], 128))

    where = jnp.stack([tensor * half, my_y, my_x])
    err, by_z = compress(own, other, used_grad, momentum, scales, where, 0)
    err, by_y, by_x = compress(own, other, used_grad, momentum, scales, where, 1, err)

    part_z = lax.psum_scatter(by_z, "z", scatter_dimension=0, tiled=True)

    from_x = turned(by_x[1], "x", 1)
    from_y = [turned(by_y[d], "y", d) for d in range(1, Y)]

    half_x = (by_x[0].astype(F32) + from_x.astype(F32)).astype(BF16)
    sum_y = by_y[0].astype(F32)
    for value in from_y:
        sum_y = sum_y + value.astype(F32)
    sent_y = turned(sum_y[1].astype(BF16), "x", 1)
    from_xy = [turned(half_x[d], "y", d) for d in range(1, Y)]
    whole_y = sum_y[0] + sent_y.astype(F32)
    whole_x = half_x[0].astype(F32)
    for value in from_xy:
        whole_x = whole_x + value.astype(F32)
    whole = jnp.concatenate([whole_y.astype(BF16), whole_x.astype(BF16)], axis=2)
    sum_b = lax.psum_scatter(whole.reshape(Z * SPAN, cut), "z", scatter_dimension=0, tiled=True)
    arrived = lax.all_to_all(
        part_z.reshape(Y * X, SPAN, cut), ("y", "x"), split_axis=0, concat_axis=0, tiled=True
    )
    sum_a = jnp.sum(arrived.astype(F32), axis=0)

    share, share_other = input_grad(used_grad, weight, 1 - tensor, by_x)
    term = other_grad[0].astype(F32) + share + turned(share_other, "tensor", 1)
    passed = lax.ppermute(term.astype(BF16), ("section", "x"), [(2, 1), (3, 0)])
    passed = lax.ppermute(passed, ("section", "x"), [(0, 1), (1, 0)])
    upstream = (term + passed.astype(F32)).astype(BF16)

    averaged = jnp.concatenate([sum_a, sum_b.astype(F32)], axis=1) / (Z * Y * X)
    server_scale = lax.psum(jnp.sum(jnp.abs(averaged)), "tensor") / (SPAN * cols * 2)
    owned = squash(averaged, server_scale)
    server_error = averaged - owned.astype(F32)

    owned_a, owned_b = owned[:, :cut], owned[:, cut:]
    all_z = lax.all_gather(owned_b, "z", axis=0, tiled=False)
    around = lax.all_to_all(
        jnp.broadcast_to(owned_a[None], (Y * X, SPAN, cut)), ("y", "x"), split_axis=0, concat_axis=0, tiled=True
    )
    all_a = lax.all_gather(around.reshape(Y * X * SPAN, cut), "z", axis=0, tiled=True)
    first_y, first_x = all_z[:, :, :COLS_Y], all_z[:, :, COLS_Y:]
    pair_y = jnp.stack([first_y, turned(first_y, "x", 1)])
    ring_x = jnp.stack([first_x] + [turned(first_x, "y", -d) for d in range(1, Y)])
    y_parts = [pair_y] + [turned(pair_y, "y", -d) for d in range(1, Y)]
    x_parts = [ring_x, turned(ring_x, "x", 1)]
    gathered = assemble(where, all_a, y_parts, x_parts)
    return (upstream[None], gathered[None], err[None, None], server_error[None])


def solution(mesh):
    sections, groups, _ = mesh.devices.shape
    fine = Mesh(mesh.devices.reshape(sections, groups, Z, Y, X), ("section", "tensor", "z", "y", "x"))
    dp = ("z", "y", "x")
    placed = (
        P("section", dp, "tensor"),
        P("section", dp, "tensor"),
        P("section", dp, "tensor"),
        P(dp),
        P("section", None, "tensor"),
        P("section", None, "tensor"),
    )
    return jax.shard_map(
        shards,
        mesh=fine,
        in_specs=placed,
        out_specs=(
            P("section", dp, "tensor"),
            P("section", None, "tensor"),
            P("section", dp, None, "tensor"),
            P("section", dp, "tensor"),
        ),
        check_vma=False,
    )
```

```python
import functools

import jax
import jax.numpy as jnp
from jax import lax
from jax.experimental import pallas as pl
from jax.experimental.pallas import tpu as pltpu
from jax.sharding import Mesh, PartitionSpec as P

momentum_decay = 0.9
saturation = 0.5
epsilon_term = 1e-06

Z, Y, X = 8, 4, 2
SPAN = 64
COLS_Y, COLS_X = 256, 256
F32, BF16 = jnp.float32, jnp.bfloat16
PARAMS = pltpu.CompilerParams(vmem_limit_bytes=32 * 1024 * 1024)
WIDE = pltpu.CompilerParams(vmem_limit_bytes=56 * 1024 * 1024)
ANY = pl.BlockSpec(memory_space=pl.ANY)
VMEM = pl.BlockSpec(memory_space=pltpu.VMEM)


def local_block(x, g, m):
    grad = lax.dot_general(x, g, (((0,), (0,)), ((), ())), preferred_element_type=F32)
    return momentum_decay * m.astype(F32) + (1.0 - momentum_decay) * grad


def local_kernel(where_ref, x_ref, g_ref, m_ref, out_ref, sums_ref):
    local = local_block(x_ref[...], g_ref[...], m_ref[...])
    out_ref[...] = local.astype(BF16)
    rows, cols = local.shape
    per_span = jnp.sum(jnp.abs(local).reshape(rows // SPAN, SPAN, cols), axis=1)
    total = per_span[:, :128]
    for lane in range(128, cols, 128):
        total = total + per_span[:, lane : lane + 128]
    sums_ref[...] = total


def masked_kernel(seqs, where_ref, x_ref, g_ref, m_ref, out_ref, sums_ref, used_ref):
    @pl.when(pl.program_id(0) == 0)
    def _():
        slots = used_ref.shape[0] // seqs
        for seq in range(seqs):
            rows = slice(seq * slots, (seq + 1) * slots)
            grads = g_ref[rows, :].astype(F32)
            slot = lax.broadcasted_iota(jnp.int32, grads.shape, 0)
            used_ref[rows, :] = jnp.where(slot < where_ref[1 + seq], grads, 0.0).astype(BF16)

    local_kernel(where_ref, x_ref, used_ref, m_ref, out_ref, sums_ref)


def local_momentum(x, g, m, first, lengths=None):
    tokens, feats = x.shape
    cols = m.shape[1]
    rows = Y * X * SPAN
    where, kernel = first.reshape(1), local_kernel
    if lengths is not None:
        where = jnp.concatenate([where, lengths])
        kernel = functools.partial(masked_kernel, lengths.shape[0])
    return pl.pallas_call(
        kernel,
        grid_spec=pltpu.PrefetchScalarGridSpec(
            num_scalar_prefetch=1,
            grid=(feats // rows,),
            in_specs=[
                pl.BlockSpec((tokens, rows), lambda i, w: (0, i)),
                pl.BlockSpec((tokens, cols), lambda i, w: (0, 0)),
                pl.BlockSpec((rows, cols), lambda i, w: (w[0] + i, 0)),
            ],
            out_specs=[
                pl.BlockSpec((rows, cols), lambda i, w: (i, 0)),
                pl.BlockSpec((rows // SPAN, 128), lambda i, w: (i, 0)),
            ]
            + ([] if lengths is None else [pl.BlockSpec((tokens, cols), lambda i, w: (0, 0))]),
        ),
        out_shape=[
            pltpu.HBM((feats, cols), BF16),
            jax.ShapeDtypeStruct((feats // SPAN, 128), F32),
        ]
        + ([] if lengths is None else [jax.ShapeDtypeStruct((tokens, cols), BF16)]),
        compiler_params=WIDE,
        cost_estimate=pl.CostEstimate(
            flops=2 * tokens * feats * cols, bytes_accessed=4 * feats * cols, transcendentals=0
        ),
    )(where, x, g, m)


def squash(local, scale):
    slope = scale / (saturation * scale + epsilon_term)
    return jnp.clip(local * slope, -scale, scale).astype(BF16)


def halves(run, own_ref, other_ref):
    half = pl.num_programs(0) // 2
    pl.when(pl.program_id(0) < half)(lambda: run(own_ref))
    pl.when(pl.program_id(0) >= half)(lambda: run(other_ref))


def compress_kernel(where_ref, own_ref, other_ref, s_ref, z_ref, *outs):
    my_y, my_x = where_ref[1], where_ref[2]
    cut = z_ref.shape[1]

    def run(local_ref):
        for k in range(Y * X):
            dy, dx = k // X, k % X
            j = lax.rem(my_y + dy, Y) * X + lax.rem(my_x + dx, X)
            rows = pl.ds(pl.multiple_of(j * SPAN, SPAN), SPAN)
            packed = squash(local_ref[rows, :].astype(F32), s_ref[pl.ds(j, 1), 0:1])
            z_ref[k * SPAN : (k + 1) * SPAN] = packed[:, :cut]
            outs[dy][dx, 0] = packed[:, cut : cut + COLS_Y]
            outs[Y + dx][dy, 0] = packed[:, cut + COLS_Y :]

    halves(run, own_ref, other_ref)


def error_kernel(where_ref, own_ref, other_ref, s_ref, after_ref, err_ref):
    def run(local_ref):
        for j in range(Y * X):
            rows = pl.ds(j * SPAN, SPAN)
            local = local_ref[rows, :].astype(F32)
            packed = squash(local, s_ref[j : j + 1, 0:1])
            err_ref[rows, :] = (local - packed.astype(F32)).astype(BF16)

    halves(run, own_ref, other_ref)


def local_specs(own):
    feats, cols = own.shape
    rows = Y * X * SPAN
    half = feats // rows

    def whole(i, w):
        return lax.rem(w[0] + i, 2 * half)

    in_specs = [
        pl.BlockSpec((rows, cols), lambda i, w: (jnp.minimum(i, half - 1), 0)),
        pl.BlockSpec((rows, cols), lambda i, w: (jnp.maximum(i - half, 0), 0)),
        pl.BlockSpec((rows // SPAN, 128), lambda i, w: (whole(i, w), 0)),
    ]
    return (2 * half,), in_specs, whole


def compress(own, other, scales, where):
    feats, cols = own.shape
    width = 2 * feats
    grid, in_specs, whole = local_specs(own)
    rows, cut = Y * X * SPAN, cols // 2
    return pl.pallas_call(
        compress_kernel,
        grid_spec=pltpu.PrefetchScalarGridSpec(
            num_scalar_prefetch=1,
            grid=grid,
            in_specs=in_specs,
            out_specs=[pl.BlockSpec((rows, cut), lambda i, w: (whole(i, w), 0))]
            + [pl.BlockSpec((X, 1, SPAN, COLS_Y), lambda i, w: (0, whole(i, w), 0, 0))] * Y
            + [pl.BlockSpec((Y, 1, SPAN, COLS_X), lambda i, w: (0, whole(i, w), 0, 0))] * X,
        ),
        out_shape=[pltpu.HBM((width, cut), BF16)]
        + [pltpu.HBM((X, Z, SPAN, COLS_Y), BF16)] * Y
        + [pltpu.HBM((Y, Z, SPAN, COLS_X), BF16)] * X,
        compiler_params=WIDE,
        cost_estimate=pl.CostEstimate(
            flops=8 * width * cols, bytes_accessed=4 * width * cols, transcendentals=0
        ),
    )(where, own, other, scales)


def compression_error(own, other, scales, where, after):
    feats, cols = own.shape
    width = 2 * feats
    grid, in_specs, whole = local_specs(own)
    return pl.pallas_call(
        error_kernel,
        grid_spec=pltpu.PrefetchScalarGridSpec(
            num_scalar_prefetch=1,
            grid=grid,
            in_specs=in_specs + [ANY],
            out_specs=pl.BlockSpec((Y * X * SPAN, cols), lambda i, w: (whole(i, w), 0)),
        ),
        out_shape=pltpu.HBM((width, cols), BF16),
        compiler_params=PARAMS,
        cost_estimate=pl.CostEstimate(
            flops=8 * width * cols, bytes_accessed=4 * width * cols, transcendentals=0
        ),
    )(where, own, other, scales, after)


def first_sums_kernel(*refs):
    kept_ref, given_ref = refs[Y + X + 1 : Y + X + 3]
    kept_ref[...] = added([ref.at[0] for ref in refs[:Y]])
    given_ref[...] = added([ref.at[1] for ref in refs[:Y]]).astype(BF16)
    for k, out_ref in enumerate(refs[Y + X + 3 : -1]):
        out_ref[...] = added([ref.at[k] for ref in refs[Y : Y + X]]).astype(BF16)


def first_sums(y_parts, x_parts, through):
    _, _, span, share_y = y_parts[0].shape
    share_x = x_parts[0].shape[3]
    return pl.pallas_call(
        first_sums_kernel,
        in_specs=[VMEM] * (Y + X) + [ANY],
        out_specs=[VMEM] * (2 + Y) + [ANY],
        out_shape=[
            jax.ShapeDtypeStruct((Z, span, share_y), F32),
            jax.ShapeDtypeStruct((Z, span, share_y), BF16),
        ]
        + [jax.ShapeDtypeStruct((Z, span, share_x), BF16)] * Y
        + [jax.ShapeDtypeStruct(through.shape, through.dtype)],
        input_output_aliases={Y + X: 2 + Y},
        compiler_params=PARAMS,
        cost_estimate=pl.CostEstimate(
            flops=16 * y_parts[0].size, bytes_accessed=20 * y_parts[0].size, transcendentals=0
        ),
    )(*y_parts, *x_parts, through)


def gathered_kernel(all_ref, swapped_ref, *refs):
    pair_ref, ring_ref = refs[-2:]
    pair_ref[0] = all_ref[:, :, :COLS_Y]
    pair_ref[1] = swapped_ref[...]
    ring_ref[0] = all_ref[:, :, COLS_Y:]
    for k in range(1, Y):
        ring_ref[k] = refs[k - 1][...]


def first_gathered(all_z, swapped, others):
    span = all_z.shape[1]
    return pl.pallas_call(
        gathered_kernel,
        in_specs=[VMEM] * (1 + Y),
        out_specs=[VMEM] * 2,
        out_shape=[
            jax.ShapeDtypeStruct((X, Z, span, COLS_Y), BF16),
            jax.ShapeDtypeStruct((Y, Z, span, COLS_X), BF16),
        ],
        compiler_params=PARAMS,
        cost_estimate=pl.CostEstimate(flops=0, bytes_accessed=8 * all_z.size, transcendentals=0),
    )(all_z, swapped, *others)


def added(refs):
    total = refs[0][...].astype(F32)
    for ref in refs[1:]:
        total = total + ref[...].astype(F32)
    return total


def plane_sum_kernel(kept_ref, other_ref, *refs):
    out_ref = refs[-1]
    out_ref[:, :, :COLS_Y] = added([kept_ref, other_ref]).astype(BF16)
    out_ref[:, :, COLS_Y:] = added(refs[:Y]).astype(BF16)


def plane_sum(kept, other, x_parts, after):
    return pl.pallas_call(
        plane_sum_kernel,
        in_specs=[VMEM] * (2 + Y) + [ANY],
        out_specs=VMEM,
        out_shape=jax.ShapeDtypeStruct((Z, SPAN, COLS_Y + COLS_X), BF16),
        compiler_params=PARAMS,
        cost_estimate=pl.CostEstimate(
            flops=8 * kept.size, bytes_accessed=12 * kept.size, transcendentals=0
        ),
    )(kept, other, *x_parts, after)


def y_sum_kernel(own_ref, *refs):
    kept_ref, given_ref = refs[-2:]
    kept_ref[...] = added([own_ref.at[0, 0]] + [ref.at[0] for ref in refs[: Y - 1]])
    given_ref[...] = added([own_ref.at[0, 1]] + [ref.at[1] for ref in refs[: Y - 1]]).astype(BF16)


def y_sum(own, parts, after):
    shape = own.shape[2:]
    return pl.pallas_call(
        y_sum_kernel,
        in_specs=[VMEM] * (1 + len(parts)) + [ANY],
        out_specs=[VMEM] * 2,
        out_shape=[jax.ShapeDtypeStruct(shape, F32), jax.ShapeDtypeStruct(shape, BF16)],
        compiler_params=PARAMS,
        cost_estimate=pl.CostEstimate(flops=own.size, bytes_accessed=3 * own.size, transcendentals=0),
    )(own, *parts, after)


def server_kernel(kept_ref, other_ref, b_ref, out_ref, sums_ref):
    cut = b_ref.shape[2]
    out_ref[:, :cut] = added([kept_ref, other_ref]) / (Z * Y * X)
    out_ref[:, cut:] = added([b_ref.at[k] for k in range(Z)]) / (Z * Y * X)
    sums_ref[...] = jnp.sum(jnp.abs(out_ref[...]), axis=0, keepdims=True)


def server_sum(kept, other, b):
    _, span, cut = b.shape
    return pl.pallas_call(
        server_kernel,
        in_specs=[VMEM] * 3,
        out_specs=[VMEM] * 2,
        out_shape=[jax.ShapeDtypeStruct((span, 2 * cut), F32), jax.ShapeDtypeStruct((1, 2 * cut), F32)],
        compiler_params=PARAMS,
        cost_estimate=pl.CostEstimate(flops=2 * b.size, bytes_accessed=5 * b.size, transcendentals=0),
    )(kept, other, b)


def owned_kernel(averaged_ref, scale_ref, error_ref, a_ref, b_ref):
    averaged = averaged_ref[...]
    owned = squash(averaged, scale_ref[...])
    error_ref[...] = averaged - owned.astype(F32)
    cut = a_ref.shape[1]
    a_ref[...] = owned[:, :cut]
    b_ref[...] = jnp.broadcast_to(owned[None, :, cut:], b_ref.shape)


def owned_momentum(averaged, scale):
    span, cols = averaged.shape
    cut = cols // 2
    return pl.pallas_call(
        owned_kernel,
        in_specs=[VMEM] * 2,
        out_specs=[VMEM] * 3,
        out_shape=[
            jax.ShapeDtypeStruct((span, cols), F32),
            jax.ShapeDtypeStruct((span, cut), BF16),
            jax.ShapeDtypeStruct((Z, span, cut), BF16),
        ],
        compiler_params=PARAMS,
        cost_estimate=pl.CostEstimate(
            flops=8 * averaged.size, bytes_accessed=24 * averaged.size, transcendentals=0
        ),
    )(averaged, scale)


def input_grad_kernel(half, where_ref, g_ref, w_ref, after_ref, own_ref, other_ref):
    step = pl.program_id(0)
    term = lax.dot_general(g_ref[...], w_ref[...], (((1,), (1,)), ((), ())), preferred_element_type=F32)

    @pl.when(step < half)
    def _():
        other_ref[...] = term.astype(BF16)

    @pl.when(step >= half)
    def _():
        own_ref[...] = term


def input_grad(g, weight, first_other, after):
    tokens, cols = g.shape
    width = weight.shape[0]
    rows = min(512, width // 2)
    half = width // 2 // rows
    return pl.pallas_call(
        functools.partial(input_grad_kernel, half),
        grid_spec=pltpu.PrefetchScalarGridSpec(
            num_scalar_prefetch=1,
            grid=(2 * half,),
            in_specs=[
                pl.BlockSpec((tokens, cols), lambda i, w: (0, 0)),
                pl.BlockSpec((rows, cols), lambda i, w: (lax.rem(w[0] * half + i, 2 * half), 0)),
                ANY,
            ],
            out_specs=[
                pl.BlockSpec((tokens, rows), lambda i, w: (0, jnp.maximum(i - half, 0))),
                pl.BlockSpec((tokens, rows), lambda i, w: (0, jnp.minimum(i, half - 1))),
            ],
        ),
        out_shape=[jax.ShapeDtypeStruct((tokens, width // 2), t) for t in (F32, BF16)],
        compiler_params=PARAMS,
        cost_estimate=pl.CostEstimate(
            flops=2 * tokens * width * cols,
            bytes_accessed=2 * width * cols + 4 * tokens * width,
            transcendentals=0,
        ),
    )(first_other.reshape(1), g, weight, after)


def copy_all(pairs, sems):
    copies = [pltpu.make_async_copy(*pair, sems.at[k]) for k, pair in enumerate(pairs)]
    for copy in copies:
        copy.start()
    for copy in copies:
        copy.wait()


def rows_of(where_ref, z, dy, dx):
    j = lax.rem(where_ref[1] + dy, Y) * X + lax.rem(where_ref[2] + dx, X)
    return pl.ds(pl.multiple_of((z * Y * X + j) * SPAN, SPAN), SPAN)


def assemble_a_kernel(where_ref, a_ref, out_ref, sems):
    cut = a_ref.shape[1]
    pairs = []
    for k in range(Z * X * Y):
        rows = rows_of(where_ref, k // (X * Y), k % Y, k // Y % X)
        pairs.append((a_ref.at[pl.ds(k * SPAN, SPAN)], out_ref.at[rows, pl.ds(0, cut)]))
    copy_all(pairs, sems)


def assemble_b_kernel(where_ref, *refs):
    out_ref, sems = refs[-2:]
    cut = out_ref.shape[1] // 2
    pairs = []
    for z in range(Z):
        for dy in range(Y):
            for dx in range(X):
                rows = rows_of(where_ref, z, dy, dx)
                pairs.append((refs[dy].at[dx, z], out_ref.at[rows, pl.ds(cut, COLS_Y)]))
                pairs.append((refs[Y + dx].at[dy, z], out_ref.at[rows, pl.ds(cut + COLS_Y, COLS_X)]))
    copy_all(pairs, sems)


def assemble(where, a, y_parts, x_parts, after):
    width, cut = a.shape

    def call(kernel, count, operands, sources, aliases):
        return pl.pallas_call(
            kernel,
            grid_spec=pltpu.PrefetchScalarGridSpec(
                num_scalar_prefetch=1,
                grid=(1,),
                in_specs=[VMEM] * sources + [ANY] * (len(operands) - sources),
                out_specs=ANY,
                scratch_shapes=[pltpu.SemaphoreType.DMA((count,))],
            ),
            out_shape=pltpu.HBM((width, 2 * cut), BF16),
            input_output_aliases=aliases,
            compiler_params=PARAMS,
            cost_estimate=pl.CostEstimate(flops=0, bytes_accessed=4 * width * cut, transcendentals=0),
        )(where, *operands)

    half = call(assemble_a_kernel, Z * Y * X, [a], 1, {})
    return call(
        assemble_b_kernel, 2 * Z * Y * X, [*y_parts, *x_parts, half, *after], Y + X, {1 + Y + X: 0}
    )


def over_tensor(value):
    return lax.ppermute(value, "tensor", [(0, 1), (1, 0)])


def along(value, axis, steps):
    count = lax.axis_size(axis)
    return lax.ppermute(value, axis, [(i, (i + steps) % count) for i in range(count)])


def exchanged(value, axes):
    return lax.all_to_all(value, axes, split_axis=0, concat_axis=0, tiled=True)


def shards(layer_input, other_grad, head_grad, lengths, proj_weight, old_momentum):
    tensor, my_y, my_x = (lax.axis_index(a).astype(jnp.int32) for a in ("tensor", "y", "x"))
    own, momentum, weight = layer_input[0], old_momentum[0], proj_weight[0]
    width, cols = momentum.shape
    cut = cols // 2
    other = over_tensor(own)

    half = width // 2 // (Y * X * SPAN)
    local_own, own_sums, used_grad = local_momentum(own, head_grad[0], momentum, tensor * half, lengths)
    local_other, other_sums = local_momentum(other, used_grad, momentum, (1 - tensor) * half)
    stacked = jnp.stack([own_sums, other_sums])
    both = jnp.where(tensor == 0, stacked, stacked[::-1]).sum(axis=2).reshape(-1)
    scales = lax.psum(both, "tensor") / (SPAN * cols * 2)
    scales = jnp.broadcast_to(scales[:, None], (scales.shape[0], 128))

    where = jnp.stack([tensor * half, my_y, my_x])
    by_z, *rest = compress(local_own, local_other, scales, where)
    part_z = lax.psum_scatter(by_z, "z", scatter_dimension=0, tiled=True)
    by_y, by_x = rest[:Y], rest[Y:]
    from_y = [by_y[0]] + [along(by_y[k], "y", k) for k in range(1, Y)]
    from_x = [by_x[0], along(by_x[1], "x", 1)]

    share, share_other = input_grad(used_grad, weight, 1 - tensor, from_y[1][0, 0, :16, :128])
    kept, given, *sum_x, share_other = first_sums(from_y, from_x, share_other)
    other_x = along(given, "x", 1)
    from_xy = [sum_x[0]] + [along(sum_x[k], "y", k) for k in range(1, Y)]
    term = other_grad[0].astype(F32) + share + over_tensor(share_other).astype(F32)
    rounded = term.astype(BF16)
    sum_plane = plane_sum(kept, other_x, from_xy, rounded)
    nearer = lax.ppermute(rounded, ("section", "x"), [(2, 1), (3, 0)])
    passed = lax.ppermute(nearer, ("section", "x"), [(0, 1), (1, 0)])
    upstream = (term + passed.astype(F32)).astype(BF16)

    arrived_b = exchanged(sum_plane, "z")
    own_a = part_z.reshape(Y, X, SPAN, cut)
    kept_a, given_a = y_sum(own_a, [along(own_a[k], "y", k) for k in range(1, Y)], nearer)
    averaged, magnitudes = server_sum(kept_a, along(given_a, "x", 1), arrived_b)

    server_scale = lax.psum(jnp.sum(magnitudes), "tensor") / (SPAN * cols * 2)
    server_error, owned_a, owned_b = owned_momentum(averaged, server_scale.reshape(1, 1))

    ring_a = jnp.concatenate([owned_a] + [along(owned_a, "y", -k) for k in range(1, Y)])
    plane_a = jnp.concatenate([ring_a, along(ring_a, "x", 1)])
    all_a = lax.all_gather(plane_a, "z", axis=0, tiled=True)
    all_z = exchanged(owned_b, "z")
    first_y, first_x = all_z[:, :, :COLS_Y], all_z[:, :, COLS_Y:]
    pair_y, ring_x = first_gathered(
        all_z, along(first_y, "x", 1), [along(first_x, "y", -k) for k in range(1, Y)]
    )
    y_parts = [pair_y] + [along(pair_y, "y", -k) for k in range(1, Y)]
    x_parts = [ring_x, along(ring_x, "x", 1)]
    err = compression_error(local_own, local_other, scales, where, pair_y)
    gathered = assemble(where, all_a, y_parts, x_parts, [upstream])
    return (upstream[None], gathered[None], err[None, None], server_error[None])


def solution(mesh):
    sections, groups, _ = mesh.devices.shape
    fine = Mesh(mesh.devices.reshape(sections, groups, Z, Y, X), ("section", "tensor", "z", "y", "x"))
    dp = ("z", "y", "x")
    placed = (
        P("section", dp, "tensor"),
        P("section", dp, "tensor"),
        P("section", dp, "tensor"),
        P(dp),
        P("section", None, "tensor"),
        P("section", None, "tensor"),
    )
    return jax.shard_map(
        shards,
        mesh=fine,
        in_specs=placed,
        out_specs=(
            P("section", dp, "tensor"),
            P("section", None, "tensor"),
            P("section", dp, None, "tensor"),
            P("section", dp, "tensor"),
        ),
        check_vma=False,
    )
```

```python
import functools

import jax
import jax.numpy as jnp
from jax import lax
from jax.experimental import pallas as pl
from jax.experimental.pallas import tpu as pltpu
from jax.sharding import Mesh, PartitionSpec as P

momentum_decay = 0.9
saturation = 0.5
epsilon_term = 1e-06

Z, Y, X = 8, 4, 2
SPAN = 64
COLS_Y, COLS_X = 256, 256
WIDE_Y, WIDE_X = 256, 256
F32, BF16 = jnp.float32, jnp.bfloat16
PARAMS = pltpu.CompilerParams(vmem_limit_bytes=32 * 1024 * 1024)
WIDE = pltpu.CompilerParams(vmem_limit_bytes=56 * 1024 * 1024)
ANY = pl.BlockSpec(memory_space=pl.ANY)
VMEM = pl.BlockSpec(memory_space=pltpu.VMEM)


def local_block(x, g, m):
    grad = lax.dot_general(x, g, (((0,), (0,)), ((), ())), preferred_element_type=F32)
    return momentum_decay * m.astype(F32) + (1.0 - momentum_decay) * grad


def local_part(x_ref, g_ref, m_ref, out_ref, sums_ref):
    local = local_block(x_ref[...], g_ref[...], m_ref[...])
    out_ref[...] = local.astype(BF16)
    rows, cols = local.shape
    per_span = jnp.sum(jnp.abs(local).reshape(rows // SPAN, SPAN, cols), axis=1)
    sums_ref[...] = in_lanes(per_span)


def in_lanes(values):
    total = values[:, :128]
    for lane in range(128, values.shape[1], 128):
        total = total + values[:, lane : lane + 128]
    return total


def own_kernel(seqs, where_ref, x_ref, g_ref, m_ref, out_ref, sums_ref, used_ref):
    @pl.when(pl.program_id(0) == 0)
    def _():
        slots = used_ref.shape[0] // seqs
        for seq in range(seqs):
            rows = slice(seq * slots, (seq + 1) * slots)
            grads = g_ref[rows, :].astype(F32)
            slot = lax.broadcasted_iota(jnp.int32, grads.shape, 0)
            used_ref[rows, :] = jnp.where(slot < where_ref[1 + seq], grads, 0.0).astype(BF16)

    local_part(x_ref, used_ref, m_ref, out_ref, sums_ref)


def other_kernel(where_ref, x_ref, g_ref, m_ref, all_sums_ref, out_ref, sums_ref):
    local_part(x_ref, g_ref, m_ref, out_ref, sums_ref)


def local_momentum(x, g, m, first, lengths=None, sums=None):
    tokens, feats = x.shape
    width, cols = m.shape
    rows = Y * X * SPAN
    where, kernel, more, used = first.reshape(1), other_kernel, [sums], []
    if lengths is not None:
        where = jnp.concatenate([where, lengths])
        kernel = functools.partial(own_kernel, lengths.shape[0])
        more, used = [], [pl.BlockSpec((tokens, cols), lambda i, w: (0, 0))]
    return pl.pallas_call(
        kernel,
        grid_spec=pltpu.PrefetchScalarGridSpec(
            num_scalar_prefetch=1,
            grid=(feats // rows,),
            in_specs=[
                pl.BlockSpec((tokens, rows), lambda i, w: (0, i)),
                pl.BlockSpec((tokens, cols), lambda i, w: (0, 0)),
                pl.BlockSpec((rows, cols), lambda i, w: (w[0] + i, 0)),
            ]
            + [ANY] * len(more),
            out_specs=[
                pl.BlockSpec((rows, cols), lambda i, w: (i, 0)),
                pl.BlockSpec((rows // SPAN, 128), lambda i, w: (w[0] + i, 0)),
            ]
            + used,
        ),
        out_shape=[
            pltpu.HBM((feats, cols), BF16),
            jax.ShapeDtypeStruct((width // SPAN, 128), F32),
        ]
        + [jax.ShapeDtypeStruct((tokens, cols), BF16)] * len(used),
        input_output_aliases={4: 1} if more else {},
        compiler_params=WIDE,
        cost_estimate=pl.CostEstimate(
            flops=2 * tokens * feats * cols, bytes_accessed=4 * feats * cols, transcendentals=0
        ),
    )(where, x, g, m, *more)


def squash(local, scale):
    slope = scale / (saturation * scale + epsilon_term)
    return jnp.clip(local * slope, -scale, scale).astype(BF16)


def halves(run, own_ref, other_ref):
    half = pl.num_programs(0) // 2
    pl.when(pl.program_id(0) < half)(lambda: run(own_ref))
    pl.when(pl.program_id(0) >= half)(lambda: run(other_ref))


def scale_of(s_ref, t_ref, rows, count):
    return jnp.sum(s_ref[rows, :] + t_ref[rows, :], axis=1, keepdims=True) / count


def compress_kernel(where_ref, own_ref, other_ref, s_ref, t_ref, z_ref, *outs):
    my_y, my_x = where_ref[1], where_ref[2]
    cut = z_ref.shape[1]

    def run(local_ref):
        for k in range(Y * X):
            dy, dx = k // X, k % X
            j = lax.rem(my_y + dy, Y) * X + lax.rem(my_x + dx, X)
            rows = pl.ds(pl.multiple_of(j * SPAN, SPAN), SPAN)
            scale = scale_of(s_ref, t_ref, pl.ds(j, 1), SPAN * local_ref.shape[1] * 2)
            packed = squash(local_ref[rows, :].astype(F32), scale)
            z_ref[k * SPAN : (k + 1) * SPAN] = packed[:, :cut]
            outs[dy][dx, 0] = packed[:, cut : cut + COLS_Y]
            outs[Y + dx][dy, 0] = packed[:, cut + COLS_Y :]

    halves(run, own_ref, other_ref)


def error_kernel(where_ref, own_ref, other_ref, s_ref, t_ref, err_ref):
    def run(local_ref):
        for j in range(Y * X):
            rows = pl.ds(j * SPAN, SPAN)
            local = local_ref[rows, :].astype(F32)
            packed = squash(local, scale_of(s_ref, t_ref, pl.ds(j, 1), SPAN * local.shape[1] * 2))
            err_ref[rows, :] = (local - packed.astype(F32)).astype(BF16)

    halves(run, own_ref, other_ref)


def local_specs(own):
    feats, cols = own.shape
    rows = Y * X * SPAN
    half = feats // rows

    def whole(i, w):
        return lax.rem(w[0] + i, 2 * half)

    in_specs = [
        pl.BlockSpec((rows, cols), lambda i, w: (jnp.minimum(i, half - 1), 0)),
        pl.BlockSpec((rows, cols), lambda i, w: (jnp.maximum(i - half, 0), 0)),
        pl.BlockSpec((rows // SPAN, 128), lambda i, w: (whole(i, w), 0)),
        pl.BlockSpec((rows // SPAN, 128), lambda i, w: (whole(i, w), 0)),
    ]
    return (2 * half,), in_specs, whole


def compress(own, other, sums, where):
    feats, cols = own.shape
    width = 2 * feats
    grid, in_specs, whole = local_specs(own)
    rows, cut = Y * X * SPAN, cols // 2
    return pl.pallas_call(
        compress_kernel,
        grid_spec=pltpu.PrefetchScalarGridSpec(
            num_scalar_prefetch=1,
            grid=grid,
            in_specs=in_specs,
            out_specs=[pl.BlockSpec((rows, cut), lambda i, w: (whole(i, w), 0))]
            + [pl.BlockSpec((X, 1, SPAN, COLS_Y), lambda i, w: (0, whole(i, w), 0, 0))] * Y
            + [pl.BlockSpec((Y, 1, SPAN, COLS_X), lambda i, w: (0, whole(i, w), 0, 0))] * X,
        ),
        out_shape=[pltpu.HBM((width, cut), BF16)]
        + [pltpu.HBM((X, Z, SPAN, COLS_Y), BF16)] * Y
        + [pltpu.HBM((Y, Z, SPAN, COLS_X), BF16)] * X,
        compiler_params=WIDE,
        cost_estimate=pl.CostEstimate(
            flops=8 * width * cols, bytes_accessed=4 * width * cols, transcendentals=0
        ),
    )(where, own, other, *sums)


def compression_error(own, other, sums, where):
    feats, cols = own.shape
    width = 2 * feats
    grid, in_specs, whole = local_specs(own)
    return pl.pallas_call(
        error_kernel,
        grid_spec=pltpu.PrefetchScalarGridSpec(
            num_scalar_prefetch=1,
            grid=grid,
            in_specs=in_specs,
            out_specs=pl.BlockSpec((Y * X * SPAN, cols), lambda i, w: (whole(i, w), 0)),
        ),
        out_shape=pltpu.HBM((width, cols), BF16),
        compiler_params=PARAMS,
        cost_estimate=pl.CostEstimate(
            flops=width, bytes_accessed=width, transcendentals=0
        ),
    )(where, own, other, *sums)


def first_sums_kernel(*refs):
    kept_ref, given_ref = refs[Y + X + 2 : Y + X + 4]
    kept_ref[...] = added([ref.at[0] for ref in refs[:Y]])
    given_ref[...] = added([ref.at[1] for ref in refs[:Y]]).astype(BF16)
    for k, out_ref in enumerate(refs[Y + X + 4 : -2]):
        out_ref[...] = added([ref.at[k] for ref in refs[Y : Y + X]]).astype(BF16)


def first_sums(y_parts, x_parts, through):
    _, _, span, share_y = y_parts[0].shape
    share_x = x_parts[0].shape[3]
    return pl.pallas_call(
        first_sums_kernel,
        in_specs=[VMEM] * (Y + X) + [ANY] * 2,
        out_specs=[VMEM] * (2 + Y) + [ANY] * 2,
        out_shape=[
            jax.ShapeDtypeStruct((Z, span, share_y), F32),
            jax.ShapeDtypeStruct((Z, span, share_y), BF16),
        ]
        + [jax.ShapeDtypeStruct((Z, span, share_x), BF16)] * Y
        + [jax.ShapeDtypeStruct(through[0].shape, through[0].dtype), pltpu.HBM(through[1].shape, through[1].dtype)],
        input_output_aliases={Y + X: 2 + Y, Y + X + 1: 3 + Y},
        compiler_params=PARAMS,
        cost_estimate=pl.CostEstimate(
            flops=16 * y_parts[0].size, bytes_accessed=20 * y_parts[0].size, transcendentals=0
        ),
    )(*y_parts, *x_parts, *through)


def pair_kernel(all_ref, swapped_ref, pair_ref):
    pair_ref[0] = all_ref[:, :, :WIDE_Y]
    pair_ref[1] = swapped_ref[...]


def ring_kernel(all_ref, *refs):
    ring_ref = refs[-1]
    ring_ref[0] = all_ref[:, :, WIDE_Y:]
    for k in range(1, Y):
        ring_ref[k] = refs[k - 1][...]


def gathered(kernel, all_z, others, share, after):
    span = all_z.shape[1]
    return pl.pallas_call(
        kernel,
        in_specs=[VMEM] * (1 + len(others)) + [ANY] * len(after),
        out_specs=VMEM,
        out_shape=jax.ShapeDtypeStruct((1 + len(others), Z, span, share), BF16),
        compiler_params=PARAMS,
        cost_estimate=pl.CostEstimate(flops=0, bytes_accessed=4 * all_z.size, transcendentals=0),
    )(all_z, *others, *after)


def added(refs):
    total = refs[0][...].astype(F32)
    for ref in refs[1:]:
        total = total + ref[...].astype(F32)
    return total


def plane_sum_kernel(kept_ref, other_ref, *refs):
    out_ref = refs[-1]
    out_ref[:, :, :COLS_Y] = added([kept_ref, other_ref]).astype(BF16)
    out_ref[:, :, COLS_Y:] = added(refs[:Y]).astype(BF16)


def plane_sum(kept, other, x_parts, after):
    return pl.pallas_call(
        plane_sum_kernel,
        in_specs=[VMEM] * (2 + Y) + [ANY],
        out_specs=VMEM,
        out_shape=jax.ShapeDtypeStruct((Z, SPAN, COLS_Y + COLS_X), BF16),
        compiler_params=PARAMS,
        cost_estimate=pl.CostEstimate(
            flops=8 * kept.size, bytes_accessed=12 * kept.size, transcendentals=0
        ),
    )(kept, other, *x_parts, after)


def y_sum_kernel(own_ref, *refs):
    kept_ref, given_ref = refs[-2:]
    kept_ref[...] = added([own_ref.at[0, 0]] + [ref.at[0] for ref in refs[: Y - 1]])
    given_ref[...] = added([own_ref.at[0, 1]] + [ref.at[1] for ref in refs[: Y - 1]]).astype(BF16)


def y_sum(own, parts, after):
    shape = own.shape[2:]
    return pl.pallas_call(
        y_sum_kernel,
        in_specs=[VMEM] * (1 + len(parts)) + [ANY],
        out_specs=[VMEM] * 2,
        out_shape=[jax.ShapeDtypeStruct(shape, F32), jax.ShapeDtypeStruct(shape, BF16)],
        compiler_params=PARAMS,
        cost_estimate=pl.CostEstimate(flops=own.size, bytes_accessed=3 * own.size, transcendentals=0),
    )(own, *parts, after)


def server_kernel(kept_ref, other_ref, b_ref, out_ref, sums_ref):
    cut = b_ref.shape[2]
    out_ref[:, :cut] = added([kept_ref, other_ref]) / (Z * Y * X)
    out_ref[:, cut:] = added([b_ref.at[k] for k in range(Z)]) / (Z * Y * X)
    rows, cols = out_ref.shape
    sums_ref[...] = in_lanes(jnp.sum(jnp.abs(out_ref[...]).reshape(rows // 8, 8, cols), axis=0))


def server_sum(kept, other, b):
    _, span, cut = b.shape
    return pl.pallas_call(
        server_kernel,
        in_specs=[VMEM] * 3,
        out_specs=[VMEM] * 2,
        out_shape=[jax.ShapeDtypeStruct((span, 2 * cut), F32), jax.ShapeDtypeStruct((8, 128), F32)],
        compiler_params=PARAMS,
        cost_estimate=pl.CostEstimate(flops=2 * b.size, bytes_accessed=5 * b.size, transcendentals=0),
    )(kept, other, b)


def owned_kernel(averaged_ref, sums_ref, other_ref, error_ref, a_ref, b_ref):
    averaged = averaged_ref[...]
    owned = squash(averaged, jnp.sum(sums_ref[...] + other_ref[...], keepdims=True) / (averaged.size * 2))
    error_ref[...] = averaged - owned.astype(F32)
    cut = a_ref.shape[1]
    a_ref[...] = owned[:, :cut]
    b_ref[...] = jnp.broadcast_to(owned[None, :, cut:], b_ref.shape)


def owned_momentum(averaged, sums, other):
    span, cols = averaged.shape
    cut = cols - WIDE_Y - WIDE_X
    return pl.pallas_call(
        owned_kernel,
        in_specs=[VMEM] * 3,
        out_specs=[VMEM] * 3,
        out_shape=[
            jax.ShapeDtypeStruct((span, cols), F32),
            jax.ShapeDtypeStruct((span, cut), BF16),
            pltpu.HBM((Z, span, cols - cut), BF16),
        ],
        compiler_params=PARAMS,
        cost_estimate=pl.CostEstimate(
            flops=8 * averaged.size, bytes_accessed=24 * averaged.size, transcendentals=0
        ),
    )(averaged, sums, other)


def input_grad_kernel(half, where_ref, g_ref, w_ref, own_ref, other_ref):
    step = pl.program_id(0)
    term = lax.dot_general(g_ref[...], w_ref[...], (((1,), (1,)), ((), ())), preferred_element_type=F32)

    @pl.when(step < half)
    def _():
        other_ref[...] = term.astype(BF16)

    @pl.when(step >= half)
    def _():
        own_ref[...] = term


def input_grad(g, weight, first_other):
    tokens, cols = g.shape
    width = weight.shape[0]
    rows = min(512, width // 2)
    half = width // 2 // rows
    return pl.pallas_call(
        functools.partial(input_grad_kernel, half),
        grid_spec=pltpu.PrefetchScalarGridSpec(
            num_scalar_prefetch=1,
            grid=(2 * half,),
            in_specs=[
                pl.BlockSpec((tokens, cols), lambda i, w: (0, 0)),
                pl.BlockSpec((rows, cols), lambda i, w: (lax.rem(w[0] * half + i, 2 * half), 0)),
            ],
            out_specs=[
                pl.BlockSpec((tokens, rows), lambda i, w: (0, jnp.maximum(i - half, 0))),
                pl.BlockSpec((tokens, rows), lambda i, w: (0, jnp.minimum(i, half - 1))),
            ],
        ),
        out_shape=[jax.ShapeDtypeStruct((tokens, width // 2), t) for t in (F32, BF16)],
        compiler_params=PARAMS,
        cost_estimate=pl.CostEstimate(
            flops=2 * tokens * width * cols,
            bytes_accessed=2 * width * cols + 4 * tokens * width,
            transcendentals=0,
        ),
    )(first_other.reshape(1), g, weight)


def copy_all(pairs, sems):
    copies = [pltpu.make_async_copy(*pair, sems.at[k]) for k, pair in enumerate(pairs)]
    for copy in copies:
        copy.start()
    for copy in copies:
        copy.wait()


def rows_of(where_ref, z, dy, dx):
    j = lax.rem(where_ref[1] + dy, Y) * X + lax.rem(where_ref[2] + dx, X)
    return pl.ds(pl.multiple_of((z * Y * X + j) * SPAN, SPAN), SPAN)


def assemble_b_kernel(y_places, x_places, cut, where_ref, *refs):
    out_ref, sems = refs[-2:]
    pairs = []
    for z in range(Z):
        for ref, dy in zip(refs, y_places):
            for dx in range(X):
                rows = rows_of(where_ref, z, dy, dx)
                pairs.append((ref.at[dx, z], out_ref.at[rows, pl.ds(cut, WIDE_Y)]))
        for ref, dx in zip(refs[len(y_places) :], x_places):
            for dy in range(Y):
                rows = rows_of(where_ref, z, dy, dx)
                pairs.append((ref.at[dy, z], out_ref.at[rows, pl.ds(cut + WIDE_Y, WIDE_X)]))
    copy_all(pairs, sems)


def assemble_a_kernel(where_ref, a_ref, _, out_ref, sems, held, held_sems):
    places, cut = X * Y, a_ref.shape[1]
    incoming, outgoing = [], []
    for z in range(Z):
        rows = pl.ds(z * places * SPAN, places * SPAN)
        incoming.append(pltpu.make_async_copy(a_ref.at[rows], held.at[rows], held_sems.at[z]))
        incoming[-1].start()
    for z in range(Z):
        incoming[z].wait()
        for k in range(z * places, (z + 1) * places):
            rows = rows_of(where_ref, z, k % Y, k // Y % X)
            source = held.at[pl.ds(k * SPAN, SPAN)]
            outgoing.append(pltpu.make_async_copy(source, out_ref.at[rows, pl.ds(0, cut)], sems.at[k]))
            outgoing[-1].start()
    for copy in outgoing:
        copy.wait()


def assemble(where, a, y_parts, x_parts, after):
    width, cut = a.shape

    def call(kernel, count, operands, space, more, scratch=()):
        return pl.pallas_call(
            kernel,
            grid_spec=pltpu.PrefetchScalarGridSpec(
                num_scalar_prefetch=1,
                grid=(1,),
                in_specs=[space] * len(operands) + [ANY] * len(more),
                out_specs=ANY,
                scratch_shapes=[pltpu.SemaphoreType.DMA((count,)), *scratch],
            ),
            out_shape=pltpu.HBM((width, cut + WIDE_Y + WIDE_X), BF16),
            input_output_aliases={1 + len(operands): 0} if more else {},
            compiler_params=PARAMS,
            cost_estimate=pl.CostEstimate(flops=0, bytes_accessed=4 * width * cut, transcendentals=0),
        )(where, *operands, *more)

    first = functools.partial(assemble_b_kernel, [0], [0], cut)
    rest = functools.partial(assemble_b_kernel, list(range(1, Y)), list(range(1, X)), cut)
    own = Z * (X + Y)
    out = call(first, own, [y_parts[0], x_parts[0]], VMEM, [])
    scratch = [pltpu.VMEM((width, cut), BF16), pltpu.SemaphoreType.DMA((Z,))]
    a = pltpu.with_memory_space_constraint(a, pltpu.HBM)
    out = call(assemble_a_kernel, Z * Y * X, [a], ANY, [out], scratch)
    return call(rest, 2 * Z * Y * X - own, [*y_parts[1:], *x_parts[1:]], VMEM, [out, *after])


def over_tensor(value):
    return lax.ppermute(value, "tensor", [(0, 1), (1, 0)])


def along(value, axis, steps):
    count = lax.axis_size(axis)
    return lax.ppermute(value, axis, [(i, (i + steps) % count) for i in range(count)])


def exchanged(value, axes):
    return lax.all_to_all(value, axes, split_axis=0, concat_axis=0, tiled=True)


def shards(layer_input, other_grad, head_grad, lengths, proj_weight, old_momentum):
    tensor, my_y, my_x = (lax.axis_index(a).astype(jnp.int32) for a in ("tensor", "y", "x"))
    own, momentum, weight = layer_input[0], old_momentum[0], proj_weight[0]
    width, cols = momentum.shape
    cut = cols // 2
    other = over_tensor(own)

    half = width // 2 // (Y * X * SPAN)
    local_own, sums, used_grad = local_momentum(own, head_grad[0], momentum, tensor * half, lengths)
    local_other, sums = local_momentum(other, used_grad, momentum, (1 - tensor) * half, sums=sums)
    sums = [sums, over_tensor(sums)]

    where = jnp.stack([tensor * half, my_y, my_x])
    by_z, *rest = compress(local_own, local_other, sums, where)
    part_z = lax.psum_scatter(by_z, "z", scatter_dimension=0, tiled=True)
    by_y, by_x = rest[:Y], rest[Y:]
    from_y = [by_y[0]] + [along(by_y[k], "y", k) for k in range(1, Y)]
    from_x = [by_x[0], along(by_x[1], "x", 1)]

    share, share_other = input_grad(used_grad, weight, 1 - tensor)
    err = compression_error(local_own, local_other, sums, where)
    kept, given, *sum_x, share_other, err = first_sums(from_y, from_x, [share_other, err])
    other_x = along(given, "x", 1)
    from_xy = [sum_x[0]] + [along(sum_x[k], "y", k) for k in range(1, Y)]
    term = other_grad[0].astype(F32) + share + over_tensor(share_other).astype(F32)
    rounded = term.astype(BF16)
    sum_plane = plane_sum(kept, other_x, from_xy, rounded[:16, :128])
    nearer = lax.ppermute(rounded, ("section", "x"), [(2, 3), (3, 2)])
    passed = lax.ppermute(nearer, ("section", "x"), [(2, 1), (3, 0)])
    upstream = (term + passed.astype(F32)).astype(BF16)

    arrived_b = exchanged(sum_plane, "z")
    own_a = part_z.reshape(Y, X, SPAN, cut)
    kept_a, given_a = y_sum(own_a, [along(own_a[k], "y", k) for k in range(1, Y)], nearer[:16, :128])
    averaged, magnitudes = server_sum(kept_a, along(given_a, "x", 1), arrived_b)

    server_error, owned_a, owned_b = owned_momentum(averaged, magnitudes, over_tensor(magnitudes))

    ring_a = jnp.concatenate([owned_a] + [along(owned_a, "y", -k) for k in range(1, Y)])
    plane_a = jnp.concatenate([ring_a, along(ring_a, "x", 1)])
    all_a = lax.all_gather(plane_a, "z", axis=0, tiled=True)
    all_z = exchanged(owned_b, "z")
    first_y, first_x = all_z[:, :, :WIDE_Y], all_z[:, :, WIDE_Y:]
    pair_y = gathered(pair_kernel, all_z, [along(first_y, "x", 1)], WIDE_Y, [])
    others = [along(first_x, "y", -k) for k in range(1, Y)]
    ring_x = gathered(ring_kernel, all_z, others, WIDE_X, [pair_y[0, 0, :16, :128]])
    y_parts = [pair_y] + [along(pair_y, "y", -k) for k in range(1, Y)]
    x_parts = [ring_x, along(ring_x, "x", 1)]
    everything = assemble(where, all_a, y_parts, x_parts, [upstream])
    return (upstream[None], everything[None], err[None, None], server_error[None])


def solution(mesh):
    sections, groups, _ = mesh.devices.shape
    fine = Mesh(mesh.devices.reshape(sections, groups, Z, Y, X), ("section", "tensor", "z", "y", "x"))
    dp = ("z", "y", "x")
    placed = (
        P("section", dp, "tensor"),
        P("section", dp, "tensor"),
        P("section", dp, "tensor"),
        P(dp),
        P("section", None, "tensor"),
        P("section", None, "tensor"),
    )
    return jax.shard_map(
        shards,
        mesh=fine,
        in_specs=placed,
        out_specs=(
            P("section", dp, "tensor"),
            P("section", None, "tensor"),
            P("section", dp, None, "tensor"),
            P("section", dp, "tensor"),
        ),
        check_vma=False,
    )
```

```python
import functools

import jax
import jax.numpy as jnp
from jax import lax
from jax.experimental import pallas as pl
from jax.experimental.pallas import tpu as pltpu
from jax.sharding import Mesh, PartitionSpec as P

momentum_decay = 0.9
saturation = 0.5
epsilon_term = 1e-06

Z, Y, X = 8, 4, 2
SPAN = 64
COLS_Y, COLS_X = 256, 256
WIDE_Y, WIDE_X = 256, 256
F32, BF16 = jnp.float32, jnp.bfloat16
PARAMS = pltpu.CompilerParams(vmem_limit_bytes=32 * 1024 * 1024)
WIDE = pltpu.CompilerParams(vmem_limit_bytes=56 * 1024 * 1024)
LESS = pltpu.CompilerParams(vmem_limit_bytes=48 * 1024 * 1024)
ANY = pl.BlockSpec(memory_space=pl.ANY)
VMEM = pl.BlockSpec(memory_space=pltpu.VMEM)


def local_block(x, g, m):
    grad = lax.dot_general(x, g, (((0,), (0,)), ((), ())), preferred_element_type=F32)
    return momentum_decay * m.astype(F32) + (1.0 - momentum_decay) * grad


def local_part(where_ref, x_ref, g_ref, m_ref, out_ref, sums_ref):
    local = local_block(x_ref[...], g_ref[...], m_ref[...])
    out_ref[...] = local.astype(BF16)
    rows, cols = local.shape
    spans = rows // SPAN
    per_span = jnp.sum(jnp.abs(local).reshape(spans, SPAN, cols), axis=1)
    at = pl.multiple_of((where_ref[0] + pl.program_id(0)) * spans, spans)
    sums_ref[pl.ds(at, spans), :] = in_lanes(per_span)


def in_lanes(values):
    total = values[:, :128]
    for lane in range(128, values.shape[1], 128):
        total = total + values[:, lane : lane + 128]
    return total


def own_kernel(where_ref, lengths_ref, x_ref, g_ref, m_ref, out_ref, sums_ref, used_ref):
    @pl.when(pl.program_id(0) == 0)
    def _():
        sums_ref[...] = jnp.zeros_like(sums_ref)
        seqs = lengths_ref.shape[0]
        slots = used_ref.shape[0] // seqs
        for seq in range(seqs):
            rows = slice(seq * slots, (seq + 1) * slots)
            grads = g_ref[rows, :].astype(F32)
            slot = lax.broadcasted_iota(jnp.int32, grads.shape, 0)
            used_ref[rows, :] = jnp.where(slot < lengths_ref[seq], grads, 0.0).astype(BF16)

    local_part(where_ref, x_ref, used_ref, m_ref, out_ref, sums_ref)


def other_kernel(where_ref, x_ref, g_ref, m_ref, all_sums_ref, out_ref, sums_ref):
    @pl.when(pl.program_id(0) == 0)
    def _():
        sums_ref[...] = all_sums_ref[...]

    local_part(where_ref, x_ref, g_ref, m_ref, out_ref, sums_ref)


def local_momentum(x, g, m, first, lengths=None, sums=None):
    tokens, feats = x.shape
    width, cols = m.shape
    rows = Y * X * SPAN
    scalars, kernel, more, used = [first.reshape(1)], other_kernel, [sums], []
    if lengths is not None:
        scalars, kernel, more = [*scalars, lengths], own_kernel, []
        used = [pl.BlockSpec((tokens, cols), lambda i, *w: (0, 0))]
    return pl.pallas_call(
        kernel,
        grid_spec=pltpu.PrefetchScalarGridSpec(
            num_scalar_prefetch=len(scalars),
            grid=(feats // rows,),
            in_specs=[
                pl.BlockSpec((tokens, rows), lambda i, *w: (0, i)),
                pl.BlockSpec((tokens, cols), lambda i, *w: (0, 0)),
                pl.BlockSpec((rows, cols), lambda i, *w: (w[0][0] + i, 0)),
            ]
            + [VMEM] * len(more),
            out_specs=[pl.BlockSpec((rows, cols), lambda i, *w: (i, 0)), VMEM] + used,
        ),
        out_shape=[
            pltpu.HBM((feats, cols), BF16),
            jax.ShapeDtypeStruct((width // SPAN, 128), F32),
        ]
        + [jax.ShapeDtypeStruct((tokens, cols), BF16)] * len(used),
        compiler_params=WIDE,
        cost_estimate=pl.CostEstimate(
            flops=2 * tokens * feats * cols, bytes_accessed=4 * feats * cols, transcendentals=0
        ),
    )(*scalars, x, g, m, *more)


def squash(local, scale):
    slope = scale / (saturation * scale + epsilon_term)
    return jnp.clip(local * slope, -scale, scale).astype(BF16)


def halves(run, own_ref, other_ref):
    half = pl.num_programs(0) // 2
    pl.when(pl.program_id(0) < half)(lambda: run(own_ref))
    pl.when(pl.program_id(0) >= half)(lambda: run(other_ref))


def scale_of(s_ref, t_ref, rows, count):
    return jnp.sum(s_ref[rows, :] + t_ref[rows, :], axis=1, keepdims=True) / count


def compress_kernel(where_ref, own_ref, other_ref, s_ref, t_ref, z_ref, *outs):
    my_y, my_x = where_ref[1], where_ref[2]
    cut = z_ref.shape[1]
    z = lax.rem(where_ref[0] + pl.program_id(0), Z)

    def run(local_ref):
        for k in range(Y * X):
            dy, dx = k // X, k % X
            j = lax.rem(my_y + dy, Y) * X + lax.rem(my_x + dx, X)
            rows = pl.ds(pl.multiple_of(j * SPAN, SPAN), SPAN)
            scale = scale_of(s_ref, t_ref, pl.ds(z * Y * X + j, 1), SPAN * local_ref.shape[1] * 2)
            packed = squash(local_ref[rows, :].astype(F32), scale)
            z_ref[k * SPAN : (k + 1) * SPAN] = packed[:, :cut]
            outs[dy][dx, 0] = packed[:, cut : cut + COLS_Y]
            outs[Y + dx][dy, 0] = packed[:, cut + COLS_Y :]

    halves(run, own_ref, other_ref)


def error_kernel(where_ref, own_ref, other_ref, s_ref, t_ref, err_ref):
    z = lax.rem(where_ref[0] + pl.program_id(0), Z)

    def run(local_ref):
        for j in range(Y * X):
            rows = pl.ds(j * SPAN, SPAN)
            local = local_ref[rows, :].astype(F32)
            scale = scale_of(s_ref, t_ref, pl.ds(z * Y * X + j, 1), SPAN * local.shape[1] * 2)
            packed = squash(local, scale)
            err_ref[rows, :] = (local - packed.astype(F32)).astype(BF16)

    halves(run, own_ref, other_ref)


def local_specs(own):
    feats, cols = own.shape
    rows = Y * X * SPAN
    half = feats // rows

    def whole(i, w):
        return lax.rem(w[0] + i, 2 * half)

    in_specs = [
        pl.BlockSpec((rows, cols), lambda i, w: (jnp.minimum(i, half - 1), 0)),
        pl.BlockSpec((rows, cols), lambda i, w: (jnp.maximum(i - half, 0), 0)),
        VMEM,
        VMEM,
    ]
    return (2 * half,), in_specs, whole


def compress(own, other, sums, where):
    feats, cols = own.shape
    width = 2 * feats
    grid, in_specs, whole = local_specs(own)
    rows, cut = Y * X * SPAN, cols // 2
    return pl.pallas_call(
        compress_kernel,
        grid_spec=pltpu.PrefetchScalarGridSpec(
            num_scalar_prefetch=1,
            grid=grid,
            in_specs=in_specs,
            out_specs=[pl.BlockSpec((rows, cut), lambda i, w: (whole(i, w), 0))]
            + [pl.BlockSpec((X, 1, SPAN, COLS_Y), lambda i, w: (0, whole(i, w), 0, 0))] * Y
            + [pl.BlockSpec((Y, 1, SPAN, COLS_X), lambda i, w: (0, whole(i, w), 0, 0))] * X,
        ),
        out_shape=[pltpu.HBM((width, cut), BF16)]
        + [pltpu.HBM((X, Z, SPAN, COLS_Y), BF16)] * Y
        + [pltpu.HBM((Y, Z, SPAN, COLS_X), BF16)] * X,
        compiler_params=LESS,
        cost_estimate=pl.CostEstimate(
            flops=8 * width * cols, bytes_accessed=4 * width * cols, transcendentals=0
        ),
    )(where, own, other, *sums)


def compression_error(own, other, sums, where):
    feats, cols = own.shape
    width = 2 * feats
    grid, in_specs, whole = local_specs(own)
    return pl.pallas_call(
        error_kernel,
        grid_spec=pltpu.PrefetchScalarGridSpec(
            num_scalar_prefetch=1,
            grid=grid,
            in_specs=in_specs,
            out_specs=pl.BlockSpec((Y * X * SPAN, cols), lambda i, w: (whole(i, w), 0)),
        ),
        out_shape=pltpu.HBM((width, cols), BF16),
        compiler_params=PARAMS,
        cost_estimate=pl.CostEstimate(
            flops=width, bytes_accessed=width, transcendentals=0
        ),
    )(where, own, other, *sums)


def first_sums_kernel(*refs):
    kept_ref, given_ref = refs[Y + X + 2 : Y + X + 4]
    kept_ref[...] = added([ref.at[0] for ref in refs[:Y]])
    given_ref[...] = added([ref.at[1] for ref in refs[:Y]]).astype(BF16)
    for k, out_ref in enumerate(refs[Y + X + 4 : -2]):
        out_ref[...] = added([ref.at[k] for ref in refs[Y : Y + X]]).astype(BF16)


def first_sums(y_parts, x_parts, through):
    _, _, span, share_y = y_parts[0].shape
    share_x = x_parts[0].shape[3]
    return pl.pallas_call(
        first_sums_kernel,
        in_specs=[VMEM] * (Y + X) + [ANY] * 2,
        out_specs=[VMEM] * (2 + Y) + [ANY] * 2,
        out_shape=[
            jax.ShapeDtypeStruct((Z, span, share_y), F32),
            jax.ShapeDtypeStruct((Z, span, share_y), BF16),
        ]
        + [jax.ShapeDtypeStruct((Z, span, share_x), BF16)] * Y
        + [jax.ShapeDtypeStruct(through[0].shape, through[0].dtype), pltpu.HBM(through[1].shape, through[1].dtype)],
        input_output_aliases={Y + X: 2 + Y, Y + X + 1: 3 + Y},
        compiler_params=PARAMS,
        cost_estimate=pl.CostEstimate(
            flops=16 * y_parts[0].size, bytes_accessed=20 * y_parts[0].size, transcendentals=0
        ),
    )(*y_parts, *x_parts, *through)


def pair_kernel(all_ref, swapped_ref, pair_ref):
    pair_ref[0] = all_ref[:, :, :WIDE_Y]
    pair_ref[1] = swapped_ref[...]


def ring_kernel(all_ref, *refs):
    ring_ref = refs[-1]
    ring_ref[0] = all_ref[:, :, WIDE_Y:]
    for k in range(1, Y):
        ring_ref[k] = refs[k - 1][...]


def gathered(kernel, all_z, others, share, after):
    span = all_z.shape[1]
    return pl.pallas_call(
        kernel,
        in_specs=[VMEM] * (1 + len(others)) + [ANY] * len(after),
        out_specs=VMEM,
        out_shape=jax.ShapeDtypeStruct((1 + len(others), Z, span, share), BF16),
        compiler_params=PARAMS,
        cost_estimate=pl.CostEstimate(flops=0, bytes_accessed=4 * all_z.size, transcendentals=0),
    )(all_z, *others, *after)


def added(refs):
    total = refs[0][...].astype(F32)
    for ref in refs[1:]:
        total = total + ref[...].astype(F32)
    return total


def plane_sum_kernel(kept_ref, other_ref, *refs):
    out_ref = refs[-1]
    out_ref[:, :, :COLS_Y] = added([kept_ref, other_ref]).astype(BF16)
    out_ref[:, :, COLS_Y:] = added(refs[:Y]).astype(BF16)


def plane_sum(kept, other, x_parts, after):
    return pl.pallas_call(
        plane_sum_kernel,
        in_specs=[VMEM] * (2 + Y) + [ANY],
        out_specs=VMEM,
        out_shape=jax.ShapeDtypeStruct((Z, SPAN, COLS_Y + COLS_X), BF16),
        compiler_params=PARAMS,
        cost_estimate=pl.CostEstimate(
            flops=8 * kept.size, bytes_accessed=12 * kept.size, transcendentals=0
        ),
    )(kept, other, *x_parts, after)


def y_sum_kernel(own_ref, *refs):
    kept_ref, given_ref = refs[-2:]
    kept_ref[...] = added([own_ref.at[0]] + [ref.at[0] for ref in refs[: Y - 1]])
    given_ref[...] = added([own_ref.at[1]] + [ref.at[1] for ref in refs[: Y - 1]]).astype(BF16)


def y_sum(own, parts, after):
    shape = own.shape[1:]
    return pl.pallas_call(
        y_sum_kernel,
        in_specs=[VMEM] * (1 + len(parts)) + [ANY],
        out_specs=[VMEM] * 2,
        out_shape=[jax.ShapeDtypeStruct(shape, F32), jax.ShapeDtypeStruct(shape, BF16)],
        compiler_params=PARAMS,
        cost_estimate=pl.CostEstimate(flops=own.size, bytes_accessed=3 * own.size, transcendentals=0),
    )(own, *parts, after)


def server_kernel(kept_ref, other_ref, b_ref, out_ref, sums_ref):
    cut = b_ref.shape[2]
    out_ref[:, :cut] = added([kept_ref, other_ref]) / (Z * Y * X)
    out_ref[:, cut:] = added([b_ref.at[k] for k in range(Z)]) / (Z * Y * X)
    rows, cols = out_ref.shape
    sums_ref[...] = in_lanes(jnp.sum(jnp.abs(out_ref[...]).reshape(rows // 8, 8, cols), axis=0))


def server_sum(kept, other, b):
    _, span, cut = b.shape
    return pl.pallas_call(
        server_kernel,
        in_specs=[VMEM] * 3,
        out_specs=[VMEM] * 2,
        out_shape=[jax.ShapeDtypeStruct((span, 2 * cut), F32), jax.ShapeDtypeStruct((8, 128), F32)],
        compiler_params=PARAMS,
        cost_estimate=pl.CostEstimate(flops=2 * b.size, bytes_accessed=5 * b.size, transcendentals=0),
    )(kept, other, b)


def owned_kernel(averaged_ref, sums_ref, other_ref, error_ref, a_ref, b_ref):
    averaged = averaged_ref[...]
    owned = squash(averaged, jnp.sum(sums_ref[...] + other_ref[...], keepdims=True) / (averaged.size * 2))
    error_ref[...] = averaged - owned.astype(F32)
    cut = a_ref.shape[1]
    a_ref[...] = owned[:, :cut]
    b_ref[...] = jnp.broadcast_to(owned[None, :, cut:], b_ref.shape)


def owned_momentum(averaged, sums, other):
    span, cols = averaged.shape
    cut = cols - WIDE_Y - WIDE_X
    return pl.pallas_call(
        owned_kernel,
        in_specs=[VMEM] * 3,
        out_specs=[VMEM] * 3,
        out_shape=[
            jax.ShapeDtypeStruct((span, cols), F32),
            jax.ShapeDtypeStruct((span, cut), BF16),
            pltpu.HBM((Z, span, cols - cut), BF16),
        ],
        compiler_params=PARAMS,
        cost_estimate=pl.CostEstimate(
            flops=8 * averaged.size, bytes_accessed=24 * averaged.size, transcendentals=0
        ),
    )(averaged, sums, other)


def input_grad_kernel(half, where_ref, g_ref, w_ref, own_ref, other_ref):
    step = pl.program_id(0)
    term = lax.dot_general(g_ref[...], w_ref[...], (((1,), (1,)), ((), ())), preferred_element_type=F32)

    @pl.when(step < half)
    def _():
        other_ref[...] = term.astype(BF16)

    @pl.when(step >= half)
    def _():
        own_ref[...] = term


def input_grad(g, weight, first_other):
    tokens, cols = g.shape
    width = weight.shape[0]
    rows = min(512, width // 2)
    half = width // 2 // rows
    return pl.pallas_call(
        functools.partial(input_grad_kernel, half),
        grid_spec=pltpu.PrefetchScalarGridSpec(
            num_scalar_prefetch=1,
            grid=(2 * half,),
            in_specs=[
                pl.BlockSpec((tokens, cols), lambda i, w: (0, 0)),
                pl.BlockSpec((rows, cols), lambda i, w: (lax.rem(w[0] * half + i, 2 * half), 0)),
            ],
            out_specs=[
                pl.BlockSpec((tokens, rows), lambda i, w: (0, jnp.maximum(i - half, 0))),
                pl.BlockSpec((tokens, rows), lambda i, w: (0, jnp.minimum(i, half - 1))),
            ],
        ),
        out_shape=[jax.ShapeDtypeStruct((tokens, width // 2), t) for t in (F32, BF16)],
        compiler_params=PARAMS,
        cost_estimate=pl.CostEstimate(
            flops=2 * tokens * width * cols,
            bytes_accessed=2 * width * cols + 4 * tokens * width,
            transcendentals=0,
        ),
    )(first_other.reshape(1), g, weight)


def copy_all(pairs, sems):
    copies = [pltpu.make_async_copy(*pair, sems.at[k]) for k, pair in enumerate(pairs)]
    for copy in copies:
        copy.start()
    for copy in copies:
        copy.wait()


def rows_of(where_ref, z, dy, dx):
    j = lax.rem(where_ref[1] + dy, Y) * X + lax.rem(where_ref[2] + dx, X)
    return pl.ds(pl.multiple_of((z * Y * X + j) * SPAN, SPAN), SPAN)


def assemble_b_kernel(y_places, x_places, cut, where_ref, *refs):
    out_ref, sems = refs[-2:]
    pairs = []
    for z in range(Z):
        for ref, dy in zip(refs, y_places):
            for dx in range(X):
                rows = rows_of(where_ref, z, dy, dx)
                pairs.append((ref.at[dx, z], out_ref.at[rows, pl.ds(cut, WIDE_Y)]))
        for ref, dx in zip(refs[len(y_places) :], x_places):
            for dy in range(Y):
                rows = rows_of(where_ref, z, dy, dx)
                pairs.append((ref.at[dy, z], out_ref.at[rows, pl.ds(cut + WIDE_Y, WIDE_X)]))
    copy_all(pairs, sems)


def assemble_a_kernel(where_ref, a_ref, _, out_ref, sems, held, held_sems):
    places, cut = X * Y, a_ref.shape[1]
    incoming, outgoing = [], []
    for z in range(Z):
        rows = pl.ds(z * places * SPAN, places * SPAN)
        incoming.append(pltpu.make_async_copy(a_ref.at[rows], held.at[rows], held_sems.at[z]))
        incoming[-1].start()
    for z in range(Z):
        incoming[z].wait()
        for k in range(z * places, (z + 1) * places):
            rows = rows_of(where_ref, z, k // X % Y, k % X)
            source = held.at[pl.ds(k * SPAN, SPAN)]
            outgoing.append(pltpu.make_async_copy(source, out_ref.at[rows, pl.ds(0, cut)], sems.at[k]))
            outgoing[-1].start()
    for copy in outgoing:
        copy.wait()


def assemble(where, a, y_parts, x_parts, after):
    width, cut = a.shape

    def call(kernel, count, operands, space, more, scratch=()):
        return pl.pallas_call(
            kernel,
            grid_spec=pltpu.PrefetchScalarGridSpec(
                num_scalar_prefetch=1,
                grid=(1,),
                in_specs=[space] * len(operands) + [ANY] * len(more),
                out_specs=ANY,
                scratch_shapes=[pltpu.SemaphoreType.DMA((count,)), *scratch],
            ),
            out_shape=pltpu.HBM((width, cut + WIDE_Y + WIDE_X), BF16),
            input_output_aliases={1 + len(operands): 0} if more else {},
            compiler_params=PARAMS,
            cost_estimate=pl.CostEstimate(flops=0, bytes_accessed=4 * width * cut, transcendentals=0),
        )(where, *operands, *more)

    first = functools.partial(assemble_b_kernel, [0], [0], cut)
    rest = functools.partial(assemble_b_kernel, list(range(1, Y)), list(range(1, X)), cut)
    own = Z * (X + Y)
    out = call(first, own, [y_parts[0], x_parts[0]], VMEM, [])
    scratch = [pltpu.VMEM((width, cut), BF16), pltpu.SemaphoreType.DMA((Z,))]
    a = pltpu.with_memory_space_constraint(a, pltpu.HBM)
    out = call(assemble_a_kernel, Z * Y * X, [a], ANY, [out], scratch)
    return call(rest, 2 * Z * Y * X - own, [*y_parts[1:], *x_parts[1:]], VMEM, [out, *after])


def over_tensor(value):
    return lax.ppermute(value, "tensor", [(0, 1), (1, 0)])


def along(value, axis, steps):
    count = lax.axis_size(axis)
    return lax.ppermute(value, axis, [(i, (i + steps) % count) for i in range(count)])


def exchanged(value, axes):
    return lax.all_to_all(value, axes, split_axis=0, concat_axis=0, tiled=True)


def shards(layer_input, other_grad, head_grad, lengths, proj_weight, old_momentum):
    tensor, my_y, my_x = (lax.axis_index(a).astype(jnp.int32) for a in ("tensor", "y", "x"))
    own, momentum, weight = layer_input[0], old_momentum[0], proj_weight[0]
    width, cols = momentum.shape
    cut = cols // 2
    other = over_tensor(own)

    half = width // 2 // (Y * X * SPAN)
    local_own, sums, used_grad = local_momentum(own, head_grad[0], momentum, tensor * half, lengths)
    local_other, sums = local_momentum(other, used_grad, momentum, (1 - tensor) * half, sums=sums)
    sums = [sums, over_tensor(sums)]

    where = jnp.stack([tensor * half, my_y, my_x])
    by_z, *rest = compress(local_own, local_other, sums, where)
    part_z = lax.psum_scatter(by_z, "z", scatter_dimension=0, tiled=True)
    by_y, by_x = rest[:Y], rest[Y:]
    from_y = [by_y[0]] + [along(by_y[k], "y", k) for k in range(1, Y)]
    from_x = [by_x[0], along(by_x[1], "x", 1)]

    share, share_other = input_grad(used_grad, weight, 1 - tensor)
    err = compression_error(local_own, local_other, sums, where)
    kept, given, *sum_x, share_other, err = first_sums(from_y, from_x, [share_other, err])
    other_x = along(given, "x", 1)
    from_xy = [sum_x[0]] + [along(sum_x[k], "y", k) for k in range(1, Y)]
    term = other_grad[0].astype(F32) + share + over_tensor(share_other).astype(F32)
    rounded = term.astype(BF16)
    sum_plane = plane_sum(kept, other_x, from_xy, rounded[:16, :128])
    nearer = lax.ppermute(rounded, ("section", "x"), [(2, 3), (3, 2)])
    passed = lax.ppermute(nearer, ("section", "x"), [(2, 1), (3, 0)])
    upstream = (term + passed.astype(F32)).astype(BF16)

    arrived_b = exchanged(sum_plane, "z")
    own_a = part_z.reshape(Y, X, SPAN, cut)
    kept_a, given_a = y_sum(own_a[0], [along(own_a[k], "y", k) for k in range(1, Y)], nearer[:16, :128])
    averaged, magnitudes = server_sum(kept_a, along(given_a, "x", 1), arrived_b)

    server_error, owned_a, owned_b = owned_momentum(averaged, magnitudes, over_tensor(magnitudes))

    pair_a = jnp.concatenate([owned_a, along(owned_a, "x", 1)])
    plane_a = jnp.concatenate([pair_a] + [along(pair_a, "y", -k) for k in range(1, Y)])
    all_a = lax.all_gather(plane_a, "z", axis=0, tiled=True)
    all_z = exchanged(owned_b, "z")
    first_y, first_x = all_z[:, :, :WIDE_Y], all_z[:, :, WIDE_Y:]
    pair_y = gathered(pair_kernel, all_z, [along(first_y, "x", 1)], WIDE_Y, [])
    others = [along(first_x, "y", -k) for k in range(1, Y)]
    ring_x = gathered(ring_kernel, all_z, others, WIDE_X, [pair_y[0, 0, :16, :128]])
    y_parts = [pair_y] + [along(pair_y, "y", -k) for k in range(1, Y)]
    x_parts = [ring_x, along(ring_x, "x", 1)]
    everything = assemble(where, all_a, y_parts, x_parts, [upstream])
    return (upstream[None], everything[None], err[None, None], server_error[None])


def solution(mesh):
    sections, groups, _ = mesh.devices.shape
    fine = Mesh(mesh.devices.reshape(sections, groups, Z, Y, X), ("section", "tensor", "z", "y", "x"))
    dp = ("z", "y", "x")
    placed = (
        P("section", dp, "tensor"),
        P("section", dp, "tensor"),
        P("section", dp, "tensor"),
        P(dp),
        P("section", None, "tensor"),
        P("section", None, "tensor"),
    )
    return jax.shard_map(
        shards,
        mesh=fine,
        in_specs=placed,
        out_specs=(
            P("section", dp, "tensor"),
            P("section", None, "tensor"),
            P("section", dp, None, "tensor"),
            P("section", dp, "tensor"),
        ),
        check_vma=False,
    )
```

```python
import functools

import jax
import jax.numpy as jnp
from jax import lax
from jax.experimental import pallas as pl
from jax.experimental.pallas import tpu as pltpu
from jax.sharding import Mesh, PartitionSpec as P

momentum_decay = 0.9
saturation = 0.5
epsilon_term = 1e-06

Z, Y, X = 8, 4, 2
SPAN = 64
COLS_Y, COLS_X = 256, 256
WIDE_Y, WIDE_X = 256, 256
F32, BF16 = jnp.float32, jnp.bfloat16
PARAMS = pltpu.CompilerParams(vmem_limit_bytes=32 * 1024 * 1024)
WIDE = pltpu.CompilerParams(vmem_limit_bytes=56 * 1024 * 1024)
LESS = pltpu.CompilerParams(vmem_limit_bytes=48 * 1024 * 1024)
ANY = pl.BlockSpec(memory_space=pl.ANY)
VMEM = pl.BlockSpec(memory_space=pltpu.VMEM)


def local_block(x, g, m):
    grad = lax.dot_general(x, g, (((0,), (0,)), ((), ())), preferred_element_type=F32)
    return momentum_decay * m.astype(F32) + (1.0 - momentum_decay) * grad


def local_part(where_ref, x_ref, g_ref, m_ref, out_ref, sums_ref):
    local = local_block(x_ref[...], g_ref[...], m_ref[...])
    out_ref[...] = local.astype(BF16)
    rows, cols = local.shape
    spans = rows // SPAN
    per_span = jnp.sum(jnp.abs(local).reshape(spans, SPAN, cols), axis=1)
    at = pl.multiple_of((where_ref[0] + pl.program_id(0)) * spans, spans)
    sums_ref[pl.ds(at, spans), :] = in_lanes(per_span)


def in_lanes(values):
    total = values[:, :128]
    for lane in range(128, values.shape[1], 128):
        total = total + values[:, lane : lane + 128]
    return total


def own_kernel(where_ref, lengths_ref, x_ref, g_ref, m_ref, out_ref, sums_ref, used_ref):
    @pl.when(pl.program_id(0) == 0)
    def _():
        sums_ref[...] = jnp.zeros_like(sums_ref)
        seqs = lengths_ref.shape[0]
        slots = used_ref.shape[0] // seqs
        for seq in range(seqs):
            rows = slice(seq * slots, (seq + 1) * slots)
            grads = g_ref[rows, :].astype(F32)
            slot = lax.broadcasted_iota(jnp.int32, grads.shape, 0)
            used_ref[rows, :] = jnp.where(slot < lengths_ref[seq], grads, 0.0).astype(BF16)

    local_part(where_ref, x_ref, used_ref, m_ref, out_ref, sums_ref)


def other_kernel(where_ref, x_ref, g_ref, m_ref, all_sums_ref, out_ref, sums_ref):
    @pl.when(pl.program_id(0) == 0)
    def _():
        sums_ref[...] = all_sums_ref[...]

    local_part(where_ref, x_ref, g_ref, m_ref, out_ref, sums_ref)


def local_momentum(x, g, m, first, lengths=None, sums=None):
    tokens, feats = x.shape
    width, cols = m.shape
    rows = Y * X * SPAN
    scalars, kernel, more, used = [first.reshape(1)], other_kernel, [sums], []
    if lengths is not None:
        scalars, kernel, more = [*scalars, lengths], own_kernel, []
        used = [pl.BlockSpec((tokens, cols), lambda i, *w: (0, 0))]
    return pl.pallas_call(
        kernel,
        grid_spec=pltpu.PrefetchScalarGridSpec(
            num_scalar_prefetch=len(scalars),
            grid=(feats // rows,),
            in_specs=[
                pl.BlockSpec((tokens, rows), lambda i, *w: (0, i)),
                pl.BlockSpec((tokens, cols), lambda i, *w: (0, 0)),
                pl.BlockSpec((rows, cols), lambda i, *w: (w[0][0] + i, 0)),
            ]
            + [VMEM] * len(more),
            out_specs=[pl.BlockSpec((rows, cols), lambda i, *w: (i, 0)), VMEM] + used,
        ),
        out_shape=[
            pltpu.HBM((feats, cols), BF16),
            jax.ShapeDtypeStruct((width // SPAN, 128), F32),
        ]
        + [jax.ShapeDtypeStruct((tokens, cols), BF16)] * len(used),
        compiler_params=WIDE,
        cost_estimate=pl.CostEstimate(
            flops=2 * tokens * feats * cols, bytes_accessed=4 * feats * cols, transcendentals=0
        ),
    )(*scalars, x, g, m, *more)


def squash(local, scale):
    slope = scale / (saturation * scale + epsilon_term)
    return jnp.clip(local * slope, -scale, scale).astype(BF16)


def halves(run, own_ref, other_ref):
    half = pl.num_programs(0) // 2
    pl.when(pl.program_id(0) < half)(lambda: run(own_ref))
    pl.when(pl.program_id(0) >= half)(lambda: run(other_ref))


def scale_of(s_ref, t_ref, rows, count):
    return jnp.sum(s_ref[rows, :] + t_ref[rows, :], axis=1, keepdims=True) / count


def compress_kernel(where_ref, own_ref, other_ref, s_ref, t_ref, z_ref, *outs):
    my_y, my_x = where_ref[1], where_ref[2]
    cut = z_ref.shape[1]
    z = lax.rem(where_ref[0] + pl.program_id(0), Z)

    def run(local_ref):
        for k in range(Y * X):
            dy, dx = k // X, k % X
            j = lax.rem(my_y + dy, Y) * X + lax.rem(my_x + dx, X)
            rows = pl.ds(pl.multiple_of(j * SPAN, SPAN), SPAN)
            scale = scale_of(s_ref, t_ref, pl.ds(z * Y * X + j, 1), SPAN * local_ref.shape[1] * 2)
            packed = squash(local_ref[rows, :].astype(F32), scale)
            z_ref[k * SPAN : (k + 1) * SPAN] = packed[:, :cut]
            outs[dy][dx, 0] = packed[:, cut : cut + COLS_Y]
            outs[Y + dx][dy, 0] = packed[:, cut + COLS_Y :]

    halves(run, own_ref, other_ref)


def error_kernel(where_ref, own_ref, other_ref, s_ref, t_ref, err_ref):
    z = lax.rem(where_ref[0] + pl.program_id(0), Z)

    def run(local_ref):
        for j in range(Y * X):
            rows = pl.ds(j * SPAN, SPAN)
            local = local_ref[rows, :].astype(F32)
            scale = scale_of(s_ref, t_ref, pl.ds(z * Y * X + j, 1), SPAN * local.shape[1] * 2)
            packed = squash(local, scale)
            err_ref[rows, :] = (local - packed.astype(F32)).astype(BF16)

    halves(run, own_ref, other_ref)


def local_specs(own):
    feats, cols = own.shape
    rows = Y * X * SPAN
    half = feats // rows

    def whole(i, w):
        return lax.rem(w[0] + i, 2 * half)

    in_specs = [
        pl.BlockSpec((rows, cols), lambda i, w: (jnp.minimum(i, half - 1), 0)),
        pl.BlockSpec((rows, cols), lambda i, w: (jnp.maximum(i - half, 0), 0)),
        VMEM,
        VMEM,
    ]
    return (2 * half,), in_specs, whole


def compress(own, other, sums, where):
    feats, cols = own.shape
    width = 2 * feats
    grid, in_specs, whole = local_specs(own)
    rows, cut = Y * X * SPAN, cols // 2
    return pl.pallas_call(
        compress_kernel,
        grid_spec=pltpu.PrefetchScalarGridSpec(
            num_scalar_prefetch=1,
            grid=grid,
            in_specs=in_specs,
            out_specs=[pl.BlockSpec((rows, cut), lambda i, w: (whole(i, w), 0))]
            + [pl.BlockSpec((X, 1, SPAN, COLS_Y), lambda i, w: (0, whole(i, w), 0, 0))] * Y
            + [pl.BlockSpec((Y, 1, SPAN, COLS_X), lambda i, w: (0, whole(i, w), 0, 0))] * X,
        ),
        out_shape=[pltpu.HBM((width, cut), BF16)]
        + [pltpu.HBM((X, Z, SPAN, COLS_Y), BF16)] * Y
        + [pltpu.HBM((Y, Z, SPAN, COLS_X), BF16)] * X,
        compiler_params=LESS,
        cost_estimate=pl.CostEstimate(
            flops=8 * width * cols, bytes_accessed=4 * width * cols, transcendentals=0
        ),
    )(where, own, other, *sums)


def compression_error(own, other, sums, where):
    feats, cols = own.shape
    width = 2 * feats
    grid, in_specs, whole = local_specs(own)
    return pl.pallas_call(
        error_kernel,
        grid_spec=pltpu.PrefetchScalarGridSpec(
            num_scalar_prefetch=1,
            grid=grid,
            in_specs=in_specs,
            out_specs=pl.BlockSpec((Y * X * SPAN, cols), lambda i, w: (whole(i, w), 0)),
        ),
        out_shape=pltpu.HBM((width, cols), BF16),
        compiler_params=PARAMS,
        cost_estimate=pl.CostEstimate(
            flops=width, bytes_accessed=width, transcendentals=0
        ),
    )(where, own, other, *sums)


def first_sums_kernel(*refs):
    kept_ref, given_ref = refs[Y + X + 2 : Y + X + 4]
    kept_ref[...] = added([ref.at[0] for ref in refs[:Y]])
    given_ref[...] = added([ref.at[1] for ref in refs[:Y]]).astype(BF16)
    for k, out_ref in enumerate(refs[Y + X + 4 : -2]):
        out_ref[...] = added([ref.at[k] for ref in refs[Y : Y + X]]).astype(BF16)


def first_sums(y_parts, x_parts, through):
    _, _, span, share_y = y_parts[0].shape
    share_x = x_parts[0].shape[3]
    return pl.pallas_call(
        first_sums_kernel,
        in_specs=[VMEM] * (Y + X) + [ANY] * 2,
        out_specs=[VMEM] * (2 + Y) + [ANY] * 2,
        out_shape=[
            jax.ShapeDtypeStruct((Z, span, share_y), F32),
            jax.ShapeDtypeStruct((Z, span, share_y), BF16),
        ]
        + [jax.ShapeDtypeStruct((Z, span, share_x), BF16)] * Y
        + [jax.ShapeDtypeStruct(through[0].shape, through[0].dtype), pltpu.HBM(through[1].shape, through[1].dtype)],
        input_output_aliases={Y + X: 2 + Y, Y + X + 1: 3 + Y},
        compiler_params=PARAMS,
        cost_estimate=pl.CostEstimate(
            flops=16 * y_parts[0].size, bytes_accessed=20 * y_parts[0].size, transcendentals=0
        ),
    )(*y_parts, *x_parts, *through)


def pair_kernel(all_ref, swapped_ref, pair_ref):
    pair_ref[0] = all_ref[:, :, :WIDE_Y]
    pair_ref[1] = swapped_ref[...]


def ring_kernel(all_ref, *refs):
    ring_ref = refs[-1]
    ring_ref[0] = all_ref[:, :, WIDE_Y:]
    for k in range(1, Y):
        ring_ref[k] = refs[k - 1][...]


def gathered(kernel, all_z, others, share, after):
    span = all_z.shape[1]
    return pl.pallas_call(
        kernel,
        in_specs=[VMEM] * (1 + len(others)) + [ANY] * len(after),
        out_specs=VMEM,
        out_shape=jax.ShapeDtypeStruct((1 + len(others), Z, span, share), BF16),
        compiler_params=PARAMS,
        cost_estimate=pl.CostEstimate(flops=0, bytes_accessed=4 * all_z.size, transcendentals=0),
    )(all_z, *others, *after)


def added(refs):
    total = refs[0][...].astype(F32)
    for ref in refs[1:]:
        total = total + ref[...].astype(F32)
    return total


def plane_sum_kernel(kept_ref, other_ref, *refs):
    out_ref = refs[-1]
    out_ref[:, :, :COLS_Y] = added([kept_ref, other_ref]).astype(BF16)
    out_ref[:, :, COLS_Y:] = added(refs[:Y]).astype(BF16)


def plane_sum(kept, other, x_parts, after):
    return pl.pallas_call(
        plane_sum_kernel,
        in_specs=[VMEM] * (2 + Y) + [ANY],
        out_specs=VMEM,
        out_shape=jax.ShapeDtypeStruct((Z, SPAN, COLS_Y + COLS_X), BF16),
        compiler_params=PARAMS,
        cost_estimate=pl.CostEstimate(
            flops=8 * kept.size, bytes_accessed=12 * kept.size, transcendentals=0
        ),
    )(kept, other, *x_parts, after)


def y_sum_kernel(own_ref, *refs):
    kept_ref, given_ref = refs[-2:]
    kept_ref[...] = added([own_ref.at[0]] + [ref.at[0] for ref in refs[: Y - 1]])
    given_ref[...] = added([own_ref.at[1]] + [ref.at[1] for ref in refs[: Y - 1]]).astype(BF16)


def y_sum(own, parts, after):
    shape = own.shape[1:]
    return pl.pallas_call(
        y_sum_kernel,
        in_specs=[VMEM] * (1 + len(parts)) + [ANY],
        out_specs=[VMEM] * 2,
        out_shape=[jax.ShapeDtypeStruct(shape, F32), jax.ShapeDtypeStruct(shape, BF16)],
        compiler_params=PARAMS,
        cost_estimate=pl.CostEstimate(flops=own.size, bytes_accessed=3 * own.size, transcendentals=0),
    )(own, *parts, after)


def server_kernel(kept_ref, other_ref, b_ref, out_ref, sums_ref):
    cut = b_ref.shape[2]
    out_ref[:, :cut] = added([kept_ref, other_ref]) / (Z * Y * X)
    out_ref[:, cut:] = added([b_ref.at[k] for k in range(Z)]) / (Z * Y * X)
    rows, cols = out_ref.shape
    sums_ref[...] = in_lanes(jnp.sum(jnp.abs(out_ref[...]).reshape(rows // 8, 8, cols), axis=0))


def server_sum(kept, other, b):
    _, span, cut = b.shape
    return pl.pallas_call(
        server_kernel,
        in_specs=[VMEM] * 3,
        out_specs=[VMEM] * 2,
        out_shape=[jax.ShapeDtypeStruct((span, 2 * cut), F32), jax.ShapeDtypeStruct((8, 128), F32)],
        compiler_params=PARAMS,
        cost_estimate=pl.CostEstimate(flops=2 * b.size, bytes_accessed=5 * b.size, transcendentals=0),
    )(kept, other, b)


def owned_kernel(averaged_ref, sums_ref, other_ref, error_ref, a_ref, b_ref):
    averaged = averaged_ref[...]
    owned = squash(averaged, jnp.sum(sums_ref[...] + other_ref[...], keepdims=True) / (averaged.size * 2))
    error_ref[...] = averaged - owned.astype(F32)
    cut = a_ref.shape[1]
    a_ref[...] = owned[:, :cut]
    b_ref[...] = jnp.broadcast_to(owned[None, :, cut:], b_ref.shape)


def owned_momentum(averaged, sums, other):
    span, cols = averaged.shape
    cut = cols - WIDE_Y - WIDE_X
    return pl.pallas_call(
        owned_kernel,
        in_specs=[VMEM] * 3,
        out_specs=[VMEM] * 3,
        out_shape=[
            jax.ShapeDtypeStruct((span, cols), F32),
            jax.ShapeDtypeStruct((span, cut), BF16),
            pltpu.HBM((Z, span, cols - cut), BF16),
        ],
        compiler_params=PARAMS,
        cost_estimate=pl.CostEstimate(
            flops=8 * averaged.size, bytes_accessed=24 * averaged.size, transcendentals=0
        ),
    )(averaged, sums, other)


def input_grad_kernel(half, where_ref, g_ref, w_ref, own_ref, other_ref):
    step = pl.program_id(0)
    term = lax.dot_general(g_ref[...], w_ref[...], (((1,), (1,)), ((), ())), preferred_element_type=F32)

    @pl.when(step < half)
    def _():
        other_ref[...] = term.astype(BF16)

    @pl.when(step >= half)
    def _():
        own_ref[...] = term


def input_grad(g, weight, first_other):
    tokens, cols = g.shape
    width = weight.shape[0]
    rows = min(512, width // 2)
    half = width // 2 // rows
    return pl.pallas_call(
        functools.partial(input_grad_kernel, half),
        grid_spec=pltpu.PrefetchScalarGridSpec(
            num_scalar_prefetch=1,
            grid=(2 * half,),
            in_specs=[
                pl.BlockSpec((tokens, cols), lambda i, w: (0, 0)),
                pl.BlockSpec((rows, cols), lambda i, w: (lax.rem(w[0] * half + i, 2 * half), 0)),
            ],
            out_specs=[
                pl.BlockSpec((tokens, rows), lambda i, w: (0, jnp.maximum(i - half, 0))),
                pl.BlockSpec((tokens, rows), lambda i, w: (0, jnp.minimum(i, half - 1))),
            ],
        ),
        out_shape=[jax.ShapeDtypeStruct((tokens, width // 2), t) for t in (F32, BF16)],
        compiler_params=PARAMS,
        cost_estimate=pl.CostEstimate(
            flops=2 * tokens * width * cols,
            bytes_accessed=2 * width * cols + 4 * tokens * width,
            transcendentals=0,
        ),
    )(first_other.reshape(1), g, weight)


def copy_all(pairs, sems):
    copies = [pltpu.make_async_copy(*pair, sems.at[k]) for k, pair in enumerate(pairs)]
    for copy in copies:
        copy.start()
    for copy in copies:
        copy.wait()


def rows_of(where_ref, z, dy, dx):
    j = lax.rem(where_ref[1] + dy, Y) * X + lax.rem(where_ref[2] + dx, X)
    return pl.ds(pl.multiple_of((z * Y * X + j) * SPAN, SPAN), SPAN)


def assemble_b_kernel(y_places, x_places, cut, where_ref, *refs):
    out_ref, sems = refs[-2:]
    pairs = []
    for z in range(Z):
        for ref, dy in zip(refs, y_places):
            for dx in range(X):
                rows = rows_of(where_ref, z, dy, dx)
                pairs.append((ref.at[dx, z], out_ref.at[rows, pl.ds(cut, WIDE_Y)]))
        for ref, dx in zip(refs[len(y_places) :], x_places):
            for dy in range(Y):
                rows = rows_of(where_ref, z, dy, dx)
                pairs.append((ref.at[dy, z], out_ref.at[rows, pl.ds(cut + WIDE_Y, WIDE_X)]))
    copy_all(pairs, sems)


def assemble_a_kernel(where_ref, a_ref, _, out_ref, sems, held, held_sems):
    places, cut = X * Y, a_ref.shape[1]
    incoming, outgoing = [], []
    for z in range(Z):
        rows = pl.ds(z * places * SPAN, places * SPAN)
        incoming.append(pltpu.make_async_copy(a_ref.at[rows], held.at[rows], held_sems.at[z]))
        incoming[-1].start()
    for z in range(Z):
        incoming[z].wait()
        for k in range(z * places, (z + 1) * places):
            rows = rows_of(where_ref, z, k // X % Y, k % X)
            source = held.at[pl.ds(k * SPAN, SPAN)]
            outgoing.append(pltpu.make_async_copy(source, out_ref.at[rows, pl.ds(0, cut)], sems.at[k]))
            outgoing[-1].start()
    for copy in outgoing:
        copy.wait()


def assemble(where, a, y_parts, x_parts, after):
    width, cut = a.shape

    def call(kernel, count, operands, space, more, scratch=()):
        return pl.pallas_call(
            kernel,
            grid_spec=pltpu.PrefetchScalarGridSpec(
                num_scalar_prefetch=1,
                grid=(1,),
                in_specs=[space] * len(operands) + [ANY] * len(more),
                out_specs=ANY,
                scratch_shapes=[pltpu.SemaphoreType.DMA((count,)), *scratch],
            ),
            out_shape=pltpu.HBM((width, cut + WIDE_Y + WIDE_X), BF16),
            input_output_aliases={1 + len(operands): 0} if more else {},
            compiler_params=PARAMS,
            cost_estimate=pl.CostEstimate(flops=0, bytes_accessed=4 * width * cut, transcendentals=0),
        )(where, *operands, *more)

    first = functools.partial(assemble_b_kernel, [0], [0], cut)
    early = functools.partial(assemble_b_kernel, [Y - 1], [], cut)
    rest = functools.partial(assemble_b_kernel, list(range(1, Y - 1)), list(range(1, X)), cut)
    own = Z * (X + Y)
    out = call(first, own, [y_parts[0], x_parts[0]], VMEM, [])
    out = call(early, Z * X, [y_parts[-1]], VMEM, [out])
    scratch = [pltpu.VMEM((width, cut), BF16), pltpu.SemaphoreType.DMA((Z,))]
    a = pltpu.with_memory_space_constraint(a, pltpu.HBM)
    out = call(assemble_a_kernel, Z * Y * X, [a], ANY, [out], scratch)
    return call(rest, 2 * Z * Y * X - own - Z * X, [*y_parts[1:-1], *x_parts[1:]], VMEM, [out, *after])


def in_vmem(value):
    return pltpu.with_memory_space_constraint(value, pltpu.VMEM)


def over_tensor(value):
    return lax.ppermute(value, "tensor", [(0, 1), (1, 0)])


def along(value, axis, steps):
    count = lax.axis_size(axis)
    return lax.ppermute(value, axis, [(i, (i + steps) % count) for i in range(count)])


def exchanged(value, axes):
    return lax.all_to_all(value, axes, split_axis=0, concat_axis=0, tiled=True)


def shards(layer_input, other_grad, head_grad, lengths, proj_weight, old_momentum):
    tensor, my_y, my_x = (lax.axis_index(a).astype(jnp.int32) for a in ("tensor", "y", "x"))
    own, momentum, weight = layer_input[0], old_momentum[0], proj_weight[0]
    width, cols = momentum.shape
    cut = cols // 2
    other = over_tensor(own)

    half = width // 2 // (Y * X * SPAN)
    local_own, sums, used_grad = local_momentum(own, head_grad[0], momentum, tensor * half, lengths)
    local_other, sums = local_momentum(in_vmem(other), used_grad, momentum, (1 - tensor) * half, sums=sums)
    sums = [sums, over_tensor(sums)]

    where = jnp.stack([tensor * half, my_y, my_x])
    by_z, *rest = compress(local_own, local_other, [in_vmem(part) for part in sums], where)
    part_z = lax.psum_scatter(by_z, "z", scatter_dimension=0, tiled=True)
    by_y, by_x = rest[:Y], rest[Y:]
    from_y = [by_y[0]] + [along(by_y[k], "y", k) for k in range(1, Y)]
    from_x = [by_x[0], along(by_x[1], "x", 1)]

    share, share_other = input_grad(used_grad, weight, 1 - tensor)
    err = compression_error(local_own, local_other, sums, where)
    kept, given, *sum_x, share_other, err = first_sums(from_y, from_x, [share_other, err])
    other_x = along(given, "x", 1)
    from_xy = [sum_x[0]] + [along(sum_x[k], "y", k) for k in range(1, Y)]
    term = other_grad[0].astype(F32) + share + over_tensor(share_other).astype(F32)
    rounded = term.astype(BF16)
    sum_plane = plane_sum(kept, other_x, from_xy, rounded[:16, :128])
    nearer = lax.ppermute(rounded, ("section", "x"), [(2, 3), (3, 2)])
    passed = lax.ppermute(nearer, ("section", "x"), [(2, 1), (3, 0)])
    upstream = (term + passed.astype(F32)).astype(BF16)

    arrived_b = exchanged(sum_plane, "z")
    own_a = part_z.reshape(Y, X, SPAN, cut)
    kept_a, given_a = y_sum(own_a[0], [along(own_a[k], "y", k) for k in range(1, Y)], nearer[:16, :128])
    averaged, magnitudes = server_sum(kept_a, along(given_a, "x", 1), arrived_b)

    server_error, owned_a, owned_b = owned_momentum(averaged, magnitudes, over_tensor(magnitudes))

    pair_a = jnp.concatenate([owned_a, along(owned_a, "x", 1)])
    plane_a = jnp.concatenate([pair_a] + [along(pair_a, "y", -k) for k in range(1, Y)])
    all_a = lax.all_gather(plane_a, "z", axis=0, tiled=True)
    all_z = exchanged(owned_b, "z")
    first_y, first_x = all_z[:, :, :WIDE_Y], all_z[:, :, WIDE_Y:]
    pair_y = gathered(pair_kernel, all_z, [along(first_y, "x", 1)], WIDE_Y, [])
    others = [along(first_x, "y", -k) for k in range(1, Y)]
    ring_x = gathered(ring_kernel, all_z, others, WIDE_X, [pair_y[0, 0, :16, :128]])
    y_parts = [pair_y] + [along(pair_y, "y", -k) for k in range(1, Y)]
    x_parts = [ring_x, along(ring_x, "x", 1)]
    everything = assemble(where, all_a, y_parts, x_parts, [upstream])
    return (upstream[None], everything[None], err[None, None], server_error[None])


def solution(mesh):
    sections, groups, _ = mesh.devices.shape
    fine = Mesh(mesh.devices.reshape(sections, groups, Z, Y, X), ("section", "tensor", "z", "y", "x"))
    dp = ("z", "y", "x")
    placed = (
        P("section", dp, "tensor"),
        P("section", dp, "tensor"),
        P("section", dp, "tensor"),
        P(dp),
        P("section", None, "tensor"),
        P("section", None, "tensor"),
    )
    return jax.shard_map(
        shards,
        mesh=fine,
        in_specs=placed,
        out_specs=(
            P("section", dp, "tensor"),
            P("section", None, "tensor"),
            P("section", dp, None, "tensor"),
            P("section", dp, "tensor"),
        ),
        check_vma=False,
    )
```
